32 devices in a mesh: dp: 32 (over z, y, x, core).
Axes of the slice: x: 2, y: 2, z: 4, core: 2. Of those that a mesh axis runs over, the one named last changes fastest.
Arguments:
- tokens: bfloat16 [4096, 3072], P('dp'), may hold values from -6 to 6
- slot_token: int32 [512], P('dp'), may hold values from 0 to 127, as said below
- slot_count: int32 [32], replicated, may hold values from 4 to 16, as said below
- slot_gate: float32 [512], P('dp'), may hold values from 0.2 to 1
- grad_out: bfloat16 [512, 3072], P('dp'), may hold values from -6 to 6
- w_gate: bfloat16 [8192, 3072], P('dp'), may hold values from -0.109375 to 0.109375
- w_up: bfloat16 [8192, 3072], P('dp'), may hold values from -0.109375 to 0.109375
- w_down: bfloat16 [8192, 3072], P('dp'), may hold values from -0.125 to 0.125
Outputs:
- expert_out: bfloat16 [512, 3072], P('dp')
- grad_rows: bfloat16 [512, 3072], P('dp')
- grad_gate_w: bfloat16 [8192, 3072], P('dp')
- grad_up_w: bfloat16 [8192, 3072], P('dp')
- grad_down_w: bfloat16 [8192, 3072], P('dp')
The draws below stay inside these ranges and needn't reach their ends.
Inputs may be any that keep to these rules, and one draw needn't show every extreme that they name: `slot_token`: the 16 slots of one device name distinct tokens of that device. `slot_count`: some device has all 16 of its slots live.
All inputs are finite; a program needn't handle non-finite values.
Results may differ from the reference program's by a relative error of at most 0.009.
Values may be sent and summed in bfloat16 or wider, within the bound.
No kernel may reach another device: no remote copies, remote signals or barrier semaphores. Data moves between devices by JAX's collectives and lax.ppermute only.
A program may use at most 128 MiB of HBM per device.

```python
import math
import jax
import jax.numpy as jnp
from jax import lax

D = 3072
FF = 8192
TOK_DEV = 128
CAP = 16
TOKENS = 4096
SLOTS = 512


def draw_slot_token(key, part):
    owners = SLOTS // CAP
    scores = jax.random.randint(key, (owners, TOK_DEV), 0, 1 << 16) * TOK_DEV + jnp.arange(TOK_DEV, dtype=jnp.int32)[None, :]
    ranking = jnp.argsort(scores, axis=1)
    return ranking[:, :CAP].reshape(-1).astype(jnp.int32)


def draw_slot_count(key, part):
    owners = SLOTS // CAP
    lowest = max(CAP // 4, 1)
    first_key, second_key = jax.random.split(key)
    counts = jax.random.randint(first_key, (owners,), lowest, CAP + 1)
    chosen = jax.random.randint(second_key, (), 0, owners)
    return jnp.where(jnp.arange(owners) == chosen, CAP, counts).astype(jnp.int32)


def shard_levels(stream_key, dims, pieces, low, high):
    def one(dim, shards_of):
        draws = jax.random.uniform(jax.random.fold_in(jax.random.fold_in(stream_key, 6), dim), (shards_of,), jnp.float32, low / len(pieces), high / len(pieces))
        return jnp.repeat(jnp.exp(draws), dims[dim] // shards_of).reshape((-1,) + (1,) * (len(dims) - dim - 1))

    gain = one(*pieces[0])
    for cut in pieces[1:]:
        gain = gain * one(*cut)
    return gain


def centred(rng, extent, deviation, most, cuts=(), held_as=jnp.bfloat16):
    level = shard_levels(rng, extent, cuts, -0.22, 0.18) if cuts else 1.0
    drawn = jax.random.normal(rng, extent, jnp.float32) * deviation * level
    return jnp.minimum(jnp.maximum(drawn, -most), most).astype(held_as)


def setup_inputs(seed: int = 0) -> dict:
    streams_of = jax.random.split(jax.random.key(seed), 9)
    tokens = centred(streams_of[0], (TOKENS, D), 1.0, 6.0, ((0, 32),))
    slot_token = draw_slot_token(jax.random.fold_in(streams_of[8], 71), 0)
    slot_count = draw_slot_count(jax.random.fold_in(streams_of[8], 71), 0)
    slot_gate = jnp.clip(0.2 + 0.8 * jax.random.uniform(streams_of[3], (SLOTS,), jnp.float32) ** shard_levels(streams_of[3], (SLOTS,), ((0, 32),), -0.2, 0.2), 0.2, 1.0)
    grad_out = centred(streams_of[4], (SLOTS, D), 1.0, 6.0, ((0, 32),))
    w_gate = centred(streams_of[5], (FF, D), D ** -0.5, 0.109375, ((0, 32),))
    w_up = centred(streams_of[6], (FF, D), D ** -0.5, 0.109375, ((0, 32),))
    w_down = centred(streams_of[7], (FF, D), (FF // 4) ** -0.5, 0.125, ((0, 32),))
    return {"tokens": tokens, "slot_token": slot_token, "slot_count": slot_count, "slot_gate": slot_gate, "grad_out": grad_out, "w_gate": w_gate, "w_up": w_up, "w_down": w_down}


def row_product(left, right):
    return lax.dot_general(left, right, (((1,), (1,)), ((), ())), preferred_element_type=jnp.float32)

def col_product(left, right):
    return lax.dot_general(left, right, (((0,), (0,)), ((), ())), preferred_element_type=jnp.float32)

def expert_pass(picked, scaled, w_gate, w_up, w_down):
    gate_pre = row_product(picked, w_gate)
    up_pre = row_product(picked, w_up)
    gate_sig = jax.nn.sigmoid(gate_pre)
    activated = gate_pre * gate_sig
    hidden = (activated * up_pre).astype(jnp.bfloat16)
    out_part = jnp.dot(hidden, w_down, preferred_element_type=jnp.float32)
    hidden_grad = row_product(scaled, w_down)
    gate_grad = (hidden_grad * up_pre * (gate_sig * (1.0 + gate_pre * (1.0 - gate_sig)))).astype(jnp.bfloat16)
    up_grad = (hidden_grad * activated).astype(jnp.bfloat16)
    row_grad = jnp.dot(gate_grad, w_gate, preferred_element_type=jnp.float32) + jnp.dot(up_grad, w_up, preferred_element_type=jnp.float32)
    grads = (col_product(gate_grad, picked), col_product(up_grad, picked), col_product(hidden, scaled))
    return (out_part, row_grad, grads)

def reference(tokens, slot_token, slot_count, slot_gate, grad_out, w_gate, w_up, w_down):
    position = jnp.arange(SLOTS, dtype=jnp.int32)
    owner = position // CAP
    picked = jnp.take(tokens, (owner * TOK_DEV + slot_token).astype(jnp.int32), axis=0)
    live_mask = position % CAP < jnp.take(slot_count, owner)
    weight = jnp.where(live_mask, slot_gate, jnp.zeros_like(slot_gate))
    scaled = (weight[:, None] * grad_out.astype(jnp.float32)).astype(jnp.bfloat16)
    out_part, row_grad, grads = expert_pass(picked, scaled, w_gate, w_up, w_down)
    factor = 1.0 / math.sqrt(SLOTS)
    expert_out = (weight[:, None] * out_part).astype(jnp.bfloat16)
    return (expert_out, row_grad.astype(jnp.bfloat16), (grads[0] * factor).astype(jnp.bfloat16), (grads[1] * factor).astype(jnp.bfloat16), (grads[2] * factor).astype(jnp.bfloat16))
```

```python
import math

import jax
import jax.numpy as jnp
from jax import lax
from jax.sharding import PartitionSpec as P

CORE, LINK_X, LINK_Y, LINK_Z = 0, 1, 2, 3
ROW_BITS = 4


def swapped(block, mask):
    count = lax.axis_size("dp")
    return lax.ppermute(block, "dp", [(low, low ^ mask) for low in range(count)])


def row_product(left, right):
    return lax.dot_general(
        left, right, (((1,), (1,)), ((), ())), preferred_element_type=jnp.float32
    )


def col_product(left, right):
    return lax.dot_general(
        left, right, (((0,), (0,)), ((), ())), preferred_element_type=jnp.float32
    )


def product(left, right):
    return jnp.dot(left, right, preferred_element_type=jnp.float32)


def half(value):
    return value.astype(jnp.bfloat16)


def plane_gather(near, first, second):
    one = swapped(near, first)
    two = swapped(near, second)
    return near, one, two, swapped(one, second)


def plane_scatter(parts, first, second):
    own, near, far, both = parts
    moved = swapped(half(jnp.concatenate([far, both], 0)), first)
    rows = own.shape[0]
    kept = near + moved[rows:]
    return own + moved[:rows] + swapped(half(kept), second)


def forward(x, panels):
    hidden, saved = [], []
    for w_gate, w_up, _ in panels:
        gate_pre = row_product(x, w_gate)
        up_pre = row_product(x, w_up)
        gate_sig = jax.nn.sigmoid(gate_pre)
        activated = gate_pre * gate_sig
        hidden.append(half(activated * up_pre))
        slope = up_pre * (gate_sig * (1.0 + gate_pre * (1.0 - gate_sig)))
        saved.append((slope, activated))
    return hidden, saved


def backward(e, panels, saved):
    gate_grad, up_grad = [], []
    for (_, _, w_down), (slope, activated) in zip(panels, saved):
        hidden_grad = row_product(e, w_down)
        gate_grad.append(half(hidden_grad * slope))
        up_grad.append(half(hidden_grad * activated))
    return gate_grad, up_grad


def summed(terms):
    total = terms[0]
    for term in terms[1:]:
        total = total + term
    return total


def shards(tokens, slot_token, slot_count, slot_gate, grad_out, w_gate, w_up, w_down):
    capacity = slot_gate.shape[0]
    devices = lax.axis_size("dp")
    all_bits = devices.bit_length() - 1
    device = lax.axis_index("dp")
    own_count = lax.dynamic_index_in_dim(slot_count, device, 0, keepdims=False)
    live_mask = jnp.arange(capacity, dtype=jnp.int32) < own_count
    weight = jnp.where(live_mask, slot_gate, 0.0)
    x_own = jnp.take(tokens, slot_token, axis=0)
    e_own = half(weight[:, None] * grad_out.astype(jnp.float32))

    core, along_x, along_y = 1 << CORE, 1 << LINK_X, 1 << LINK_Y
    levels = range(1 << (ROW_BITS + 1 - LINK_Z))
    far_bits = range(ROW_BITS + 1, all_bits)

    x_level = [x_own] + [swapped(x_own, k << LINK_Z) for k in levels[1:]]
    e_level = [e_own] + [swapped(e_own, k << LINK_Z) for k in levels[1:]]
    groups = [levels[:2], levels[2:]]

    near = [w_gate, w_up, w_down]
    for bit in far_bits:
        near = [jnp.concatenate([w, swapped(w, 1 << bit)], 0) for w in near]
    panels = [near, [swapped(w, core) for w in near]]

    x_rows, e_rows, hiddens, gate_grads, up_grads = [], [], [], [], []
    sums = {}
    for group in groups:
        x_near = jnp.concatenate([x_level[k] for k in group], 0)
        e_near = jnp.concatenate([e_level[k] for k in group], 0)
        x_plane = plane_gather(x_near, along_x, along_y)
        e_plane = plane_gather(e_near, along_y, along_x)
        x = jnp.concatenate(x_plane, 0)
        e = jnp.concatenate([e_plane[0], e_plane[2], e_plane[1], e_plane[3]], 0)
        hidden, saved = forward(x, panels)
        gate_grad, up_grad = backward(e, panels, saved)
        out_part = summed([product(h, p[2]) for h, p in zip(hidden, panels)])
        row_part = summed(
            [product(g, p[0]) + product(u, p[1]) for g, u, p in zip(gate_grad, up_grad, panels)]
        )
        rows = x_near.shape[0]
        out_parts = [out_part[i * rows : (i + 1) * rows] for i in range(4)]
        row_parts = [row_part[i * rows : (i + 1) * rows] for i in (0, 2, 1, 3)]
        out_sum = plane_scatter(out_parts, along_y, along_x)
        row_sum = plane_scatter(row_parts, along_x, along_y)
        for i, k in enumerate(group):
            sums[k] = (
                out_sum[i * capacity : (i + 1) * capacity],
                row_sum[i * capacity : (i + 1) * capacity],
            )
        x_rows.append(x)
        e_rows.append(e)
        hiddens.append(hidden)
        gate_grads.append(gate_grad)
        up_grads.append(up_grad)

    out_own, row_own = sums[0]
    for k in levels[1:]:
        out_own = out_own + swapped(half(sums[k][0]), k << LINK_Z)
        row_own = row_own + swapped(half(sums[k][1]), k << LINK_Z)

    x_all = jnp.concatenate(x_rows, 0)
    e_all = jnp.concatenate(e_rows, 0)
    owned = []
    for left, right in ((gate_grads, x_all), (up_grads, x_all), (hiddens, e_all)):
        mine, other = (
            col_product(jnp.concatenate([part[i] for part in left], 0), right) for i in (0, 1)
        )
        total = mine + swapped(half(other), core)
        for bit in reversed(far_bits):
            middle = total.shape[0] // 2
            total = total[:middle] + swapped(half(total[middle:]), 1 << bit)
        owned.append(total)
    factor = 1.0 / math.sqrt(devices * capacity)
    return (
        half(weight[:, None] * out_own),
        half(row_own),
        half(owned[0] * factor),
        half(owned[1] * factor),
        half(owned[2] * factor),
    )


def solution(mesh):
    return jax.shard_map(
        shards,
        mesh=mesh,
        in_specs=(
            P("dp", None),
            P("dp"),
            P(),
            P("dp"),
            P("dp", None),
            P("dp", None),
            P("dp", None),
            P("dp", None),
        ),
        out_specs=(P("dp", None), P("dp", None), P("dp", None), P("dp", None), P("dp", None)),
        check_vma=False,
    )
```

```python
import functools
import math

import jax
import jax.numpy as jnp
from jax import lax
from jax.experimental import pallas as pl
from jax.experimental.pallas import tpu as pltpu
from jax.sharding import PartitionSpec as P

CORE, LINK_X, LINK_Y, LINK_Z = 0, 1, 2, 3
ROW_BITS = 4
PANEL = 512
TURN = pltpu.VMEM((8, 128), jnp.float32)
VMEM = pl.BlockSpec(memory_space=pltpu.VMEM)
HBM = pl.BlockSpec(memory_space=pltpu.HBM)
SMEM = pl.BlockSpec(memory_space=pltpu.SMEM)


def swapped(block, mask):
    count = lax.axis_size("dp")
    return lax.ppermute(block, "dp", [(low, low ^ mask) for low in range(count)])


def row_product(left, right):
    return lax.dot_general(
        left, right, (((1,), (1,)), ((), ())), preferred_element_type=jnp.float32
    )


def col_product(left, right):
    return lax.dot_general(
        left, right, (((0,), (0,)), ((), ())), preferred_element_type=jnp.float32
    )


def product(left, right):
    return jnp.dot(left, right, preferred_element_type=jnp.float32)


def half(value):
    return value.astype(jnp.bfloat16)


def shape(dims, dtype=jnp.bfloat16):
    return jax.ShapeDtypeStruct(dims, dtype)


def held(dims, dtype=jnp.bfloat16):
    return pltpu.VMEM(dims, dtype)


def fetched(*values):
    return [pltpu.with_memory_space_constraint(value, pltpu.VMEM) for value in values]


def in_hbm(value):
    return pltpu.with_memory_space_constraint(value, pltpu.HBM)


def limit(mib):
    return pltpu.CompilerParams(vmem_limit_bytes=mib << 20)


def cost(flops, moved):
    return pl.CostEstimate(flops=flops, bytes_accessed=moved, transcendentals=0)


def pick_kernel(
    place, token, count, gate, tokens, grad, w_gate, w_up, w_down, rows, weight, panels, turn,
    token_here, count_here, gate_here, tokens_here, grad_here, arrived,
):
    pairs = (
        (token, token_here),
        (count, count_here),
        (gate, gate_here),
        (tokens, tokens_here),
        (grad, grad_here),
    )
    copies = [pltpu.make_async_copy(*pair, arrived.at[i]) for i, pair in enumerate(pairs)]
    loads = [
        pltpu.make_async_copy(w, panels.at[i], arrived.at[len(pairs) + i])
        for i, w in enumerate((w_gate, w_up, w_down))
    ]
    for copy in copies + loads:
        copy.start()
    turn[...] = jnp.zeros_like(turn)
    for copy in copies:
        copy.wait()
    capacity, lanes = weight.shape
    row = lax.broadcasted_iota(jnp.int32, (capacity, lanes), 0)
    live = count_here[place[0]]
    index = jnp.zeros((capacity, lanes), jnp.int32)
    scale = jnp.zeros((capacity, lanes), jnp.float32)
    for slot in range(capacity):
        index = jnp.where(row == slot, token_here[slot], index)
        scale = jnp.where(row == slot, jnp.where(slot < live, gate_here[slot], 0.0), scale)
    weight[...] = scale
    lane = lax.broadcasted_iota(jnp.int32, (capacity, tokens.shape[0]), 1)
    chosen = jnp.where(lane == index[:, :1], 1.0, 0.0).astype(jnp.bfloat16)
    rows[0] = half(product(chosen, tokens_here[...]))
    rows[1] = half(scale[:, :1] * grad_here[...].astype(jnp.float32))
    for copy in loads:
        copy.wait()


def pick(tokens, slot_token, slot_count, slot_gate, grad_out, weights):
    capacity, width = grad_out.shape
    inputs = (slot_token, slot_count, slot_gate, tokens, grad_out)
    return pl.pallas_call(
        pick_kernel,
        out_shape=(
            held((2, capacity, width)),
            held((capacity, 128), jnp.float32),
            held((3, *weights[0].shape)),
            TURN,
        ),
        in_specs=[SMEM] + [HBM] * 8,
        out_specs=(VMEM,) * 4,
        scratch_shapes=[pltpu.SMEM(v.shape, v.dtype) for v in inputs[:3]]
        + [pltpu.VMEM(v.shape, v.dtype) for v in inputs[3:]]
        + [pltpu.SemaphoreType.DMA((8,))],
        compiler_params=limit(4),
        cost_estimate=cost(0, 0),
        name="pick",
    )(lax.axis_index("dp")[None], *(in_hbm(v) for v in (*inputs, *weights)))


def expert_kernel(
    x_pair, x_far, e_pair, e_far, near, other, _,
    x, e, hidden, gate_grad, up_grad, out_keep, out_send, row_keep, row_send, turn,
):
    turn[...] = jnp.zeros_like(turn)
    units = near.shape[1]
    rows = x.shape[0] // 4
    x[: 2 * rows] = x_pair[...]
    x[2 * rows :] = x_far[...]
    e[:rows] = e_pair[:rows]
    e[rows : 2 * rows] = e_far[:rows]
    e[2 * rows : 3 * rows] = e_pair[rows:]
    e[3 * rows :] = e_far[rows:]
    for i, panels in enumerate((near, other)):
        mine = slice(i * units, (i + 1) * units)
        gate_pre = row_product(x[...], panels[0])
        up_pre = row_product(x[...], panels[1])
        hidden_grad = row_product(e[...], panels[2])
        gate_sig = jax.nn.sigmoid(gate_pre)
        activated = gate_pre * gate_sig
        hidden[:, mine] = half(activated * up_pre)
        gate_grad[:, mine] = half(
            hidden_grad * up_pre * (gate_sig * (1.0 + gate_pre * (1.0 - gate_sig)))
        )
        up_grad[:, mine] = half(hidden_grad * activated)
    for at in range(0, x.shape[1], PANEL):
        part = slice(at, at + PANEL)
        out = product(hidden[:, :units], near[2, :, part]) + product(
            hidden[:, units:], other[2, :, part]
        )
        out_keep[:, part] = out[: 2 * rows]
        out_send[:, part] = half(out[2 * rows :])
        row = (
            product(gate_grad[:, :units], near[0, :, part])
            + product(gate_grad[:, units:], other[0, :, part])
            + product(up_grad[:, :units], near[1, :, part])
            + product(up_grad[:, units:], other[1, :, part])
        )
        row_keep[:rows, part] = row[:rows]
        row_keep[rows:, part] = row[2 * rows : 3 * rows]
        row_send[:rows, part] = half(row[rows : 2 * rows])
        row_send[rows:, part] = half(row[3 * rows :])


def expert(x_pair, x_far, e_pair, e_far, near, other, turn):
    rows, width = 2 * x_pair.shape[0], x_pair.shape[1]
    units = 2 * near.shape[1]
    saved, kept, sent = (
        held((rows, units)),
        held((rows // 2, width), jnp.float32),
        held((rows // 2, width)),
    )
    return pl.pallas_call(
        expert_kernel,
        out_shape=(held((rows, width)),) * 2 + (saved,) * 3 + (kept, sent, kept, sent, TURN),
        in_specs=[VMEM] * 7,
        out_specs=(VMEM,) * 10,
        compiler_params=limit(12),
        cost_estimate=cost(12 * rows * units * width, 6 * units * width),
        name="expert",
    )(*fetched(x_pair, x_far, e_pair, e_far, near, other, turn))


def other_kernel(x, e, hidden, gate_grad, up_grad, _, grads, turn):
    turn[...] = jnp.zeros_like(turn)
    units = hidden.shape[1] // 2
    grads[0] = half(col_product(gate_grad[:, units:], x[...]))
    grads[1] = half(col_product(up_grad[:, units:], x[...]))
    grads[2] = half(col_product(hidden[:, units:], e[...]))


def other_grads(x, e, hidden, gate_grad, up_grad, turn):
    rows, width = x.shape
    units = hidden.shape[1] // 2
    wide = pl.BlockSpec((rows, PANEL), lambda i: (0, i))
    return pl.pallas_call(
        other_kernel,
        grid=(width // PANEL,),
        out_shape=(held((3, units, width)), TURN),
        in_specs=[wide, wide, VMEM, VMEM, VMEM, VMEM],
        out_specs=(pl.BlockSpec((3, units, PANEL), lambda i: (0, 0, i)), VMEM),
        compiler_params=limit(16),
        cost_estimate=cost(6 * rows * units * width, 6 * units * width),
        name="other_grads",
    )(*fetched(x, e, hidden, gate_grad, up_grad, turn))


def own_kernel(factor, x, e, hidden, gate_grad, up_grad, received, _, *grads):
    grads, turn = grads[:3], grads[3]
    turn[...] = jnp.zeros_like(turn)
    units = hidden.shape[1] // 2
    for i, (left, right) in enumerate(((gate_grad, x), (up_grad, x), (hidden, e))):
        total = col_product(left[:, :units], right[...]) + received[i].astype(jnp.float32)
        grads[i][...] = (total * factor).astype(grads[i].dtype)


def own_grads(x, e, hidden, gate_grad, up_grad, received, turn, factor, dtype):
    rows, width = x.shape
    units = hidden.shape[1] // 2
    wide = pl.BlockSpec((rows, PANEL), lambda i: (0, i))
    block = pl.BlockSpec((units, PANEL), lambda i: (0, i))
    return pl.pallas_call(
        functools.partial(own_kernel, factor),
        grid=(width // PANEL,),
        out_shape=(shape((units, width), dtype),) * 3 + (TURN,),
        in_specs=[wide, wide, VMEM, VMEM, VMEM]
        + [pl.BlockSpec((3, units, PANEL), lambda i: (0, 0, i)), VMEM],
        out_specs=(block,) * 3 + (VMEM,),
        compiler_params=limit(16),
        cost_estimate=cost(6 * rows * units * width, 6 * units * width),
        name="own_grads",
    )(*fetched(x, e, hidden, gate_grad, up_grad, received, turn))


def staged(body, name, outs, *values):
    def kernel(*refs):
        refs[-1][...] = jnp.zeros(TURN.shape, TURN.dtype)
        body(*refs[: len(values) - 1], *refs[len(values) : -1])

    return pl.pallas_call(
        kernel,
        out_shape=(*outs, TURN),
        in_specs=[VMEM] * len(values),
        out_specs=(VMEM,) * (len(outs) + 1),
        compiler_params=limit(4),
        cost_estimate=cost(0, 0),
        name=name,
    )(*fetched(*values))


def split_body(first, second, x, e):
    rows = first.shape[1]
    for out, i in ((x, 0), (e, 1)):
        out[:rows] = first[i]
        out[rows:] = second[i]


def pair_body(x, x_side, e, e_side, x_pair, e_pair):
    rows = x.shape[0]
    for out, near, side in ((x_pair, x, x_side), (e_pair, e, e_side)):
        out[:rows] = near[...]
        out[rows:] = side[...]


def plane_body(out_keep, out_far, row_keep, row_far, out_mid, out_side, row_mid, row_side):
    rows = out_mid.shape[0]
    for keep, far, mid, side in (
        (out_keep, out_far, out_mid, out_side),
        (row_keep, row_far, row_mid, row_side),
    ):
        mid[...] = keep[:rows] + far[:rows].astype(jnp.float32)
        side[...] = half(keep[rows:] + far[rows:].astype(jnp.float32))


def line_body(out_mid, out_side, row_mid, row_side, first, second):
    rows = first.shape[1]
    for i, (mid, side) in enumerate(((out_mid, out_side), (row_mid, row_side))):
        total = mid[...] + side[...].astype(jnp.float32)
        first[i] = total[:rows].astype(first.dtype)
        second[i] = total[rows:].astype(second.dtype)


def final_body(own, one, two, three, weight, expert_out, grad_rows):
    out, row = (
        own[i] + one[i].astype(jnp.float32) + two[i].astype(jnp.float32) + three[i].astype(jnp.float32)
        for i in (0, 1)
    )
    expert_out[...] = half(weight[:, :1] * out)
    grad_rows[...] = half(row)


def shards(tokens, slot_token, slot_count, slot_gate, grad_out, w_gate, w_up, w_down):
    capacity = slot_gate.shape[0]
    devices = lax.axis_size("dp")
    all_bits = devices.bit_length() - 1
    core, along_x, along_y = 1 << CORE, 1 << LINK_X, 1 << LINK_Y
    levels = range(1 << (ROW_BITS + 1 - LINK_Z))
    far_bits = range(ROW_BITS + 1, all_bits)

    weights = [w_gate, w_up, w_down]
    for bit in far_bits:
        weights = [jnp.concatenate([w, swapped(w, 1 << bit)], 0) for w in weights]
    own, weight, near, turn = pick(tokens, slot_token, slot_count, slot_gate, grad_out, weights)
    other = swapped(near, core)

    level = [own] + [None] * (len(levels) - 1)
    groups = [(1, 3), (0, 2)]
    for k in (1, 3, 2):
        level[k] = swapped(own, k << LINK_Z)

    width = own.shape[2]
    rows = 2 * capacity
    near_rows, pairs, works, sides = [], [], [], []
    for first, second in groups:
        x, e, turn = staged(
            split_body, "split", [held((rows, width))] * 2, level[first], level[second], turn
        )
        near_rows.append((x, swapped(x, along_x), e, swapped(e, along_y)))
    for group in near_rows:
        x, e, turn = staged(pair_body, "pair", [held((2 * rows, width))] * 2, *group, turn)
        pairs.append((x, swapped(x, along_y), e, swapped(e, along_x)))
    for group in pairs:
        *work, out_keep, out_send, row_keep, row_send, _ = expert(*group, near, other, turn)
        works.append(work)
        sides.append((out_keep, swapped(out_send, along_y), row_keep, swapped(row_send, along_x)))
    kept = [jnp.concatenate(pieces, 0) for pieces in zip(*works)]
    sent, turn = other_grads(*kept, turn)
    received = swapped(sent, core)

    whole, piece = held((rows, width), jnp.float32), held((rows, width))

    def plane_sum(side, turn):
        out_mid, out_side, row_mid, row_side, turn = staged(
            plane_body, "plane_sum", [whole, piece, whole, piece], *side, turn
        )
        return (out_mid, swapped(out_side, along_x), row_mid, swapped(row_side, along_y)), turn

    def line_sum(middle, turn, first):
        level_dims = (2, capacity, width)
        return staged(
            line_body, "line_sum", [held(level_dims, first), held(level_dims)], *middle, turn
        )

    middles = []
    for side in sides:
        middle, turn = plane_sum(side, turn)
        middles.append(middle)
    sum_1, sum_3, turn = line_sum(middles[0], turn, jnp.bfloat16)
    one, three = swapped(sum_1, 1 << LINK_Z), swapped(sum_3, 3 << LINK_Z)
    factor = 1.0 / math.sqrt(devices * capacity)
    if far_bits:
        *owned, turn = own_grads(*kept, received, turn, 1.0, jnp.float32)
        for bit in reversed(far_bits):
            cut = owned[0].shape[0] // 2
            owned = [t[:cut] + swapped(half(t[cut:]), 1 << bit) for t in owned]
        owned = [half(total * factor) for total in owned]
    else:
        *owned, turn = own_grads(*kept, received, turn, factor, jnp.bfloat16)
    sum_0, sum_2, turn = line_sum(middles[1], turn, jnp.float32)
    two = swapped(sum_2, 2 << LINK_Z)
    expert_out, grad_rows, turn = staged(
        final_body, "final", [shape((capacity, width))] * 2, sum_0, one, two, three, weight, turn
    )
    return (expert_out, grad_rows, *owned)


def solution(mesh):
    return jax.shard_map(
        shards,
        mesh=mesh,
        in_specs=(
            P("dp", None),
            P("dp"),
            P(),
            P("dp"),
            P("dp", None),
            P("dp", None),
            P("dp", None),
            P("dp", None),
        ),
        out_specs=(P("dp", None), P("dp", None), P("dp", None), P("dp", None), P("dp", None)),
        check_vma=False,
    )
```

```python
import functools
import math

import jax
import jax.numpy as jnp
from jax import lax
from jax.experimental import pallas as pl
from jax.experimental.pallas import tpu as pltpu
from jax.sharding import PartitionSpec as P

CORE, LINK_X, LINK_Y, LINK_Z = 0, 1, 2, 3
ROW_BITS = 4
LONG = 10**11
PANEL = 512
TURN = pltpu.VMEM((8, 128), jnp.float32)
VMEM = pl.BlockSpec(memory_space=pltpu.VMEM)
HBM = pl.BlockSpec(memory_space=pltpu.HBM)
SMEM = pl.BlockSpec(memory_space=pltpu.SMEM)


def swapped(block, mask):
    count = lax.axis_size("dp")
    return lax.ppermute(block, "dp", [(low, low ^ mask) for low in range(count)])


def row_product(left, right):
    return lax.dot_general(
        left, right, (((1,), (1,)), ((), ())), preferred_element_type=jnp.float32
    )


def col_product(left, right):
    return lax.dot_general(
        left, right, (((0,), (0,)), ((), ())), preferred_element_type=jnp.float32
    )


def product(left, right):
    return jnp.dot(left, right, preferred_element_type=jnp.float32)


def half(value):
    return value.astype(jnp.bfloat16)


def shape(dims, dtype=jnp.bfloat16):
    return jax.ShapeDtypeStruct(dims, dtype)


def held(dims, dtype=jnp.bfloat16):
    return pltpu.VMEM(dims, dtype)


def fetched(*values):
    return [pltpu.with_memory_space_constraint(value, pltpu.VMEM) for value in values]


def in_hbm(value):
    return pltpu.with_memory_space_constraint(value, pltpu.HBM)


def limit(mib):
    return pltpu.CompilerParams(vmem_limit_bytes=mib << 20)


def cost(flops, moved):
    return pl.CostEstimate(flops=flops, bytes_accessed=moved, transcendentals=0)


def pick_kernel(
    place, token, count, gate, tokens, grad, rows, x, e, weight, turn,
    token_here, count_here, gate_here, tokens_here, grad_here, arrived,
):
    pairs = (
        (token, token_here),
        (count, count_here),
        (gate, gate_here),
        (tokens, tokens_here),
        (grad, grad_here),
    )
    copies = [pltpu.make_async_copy(*pair, arrived.at[i]) for i, pair in enumerate(pairs)]
    for copy in copies:
        copy.start()
    turn[...] = jnp.zeros_like(turn)
    for copy in copies:
        copy.wait()
    capacity, lanes = weight.shape
    row = lax.broadcasted_iota(jnp.int32, (capacity, lanes), 0)
    live = count_here[place[0]]
    index = jnp.zeros((capacity, lanes), jnp.int32)
    scale = jnp.zeros((capacity, lanes), jnp.float32)
    for slot in range(capacity):
        index = jnp.where(row == slot, token_here[slot], index)
        scale = jnp.where(row == slot, jnp.where(slot < live, gate_here[slot], 0.0), scale)
    weight[...] = scale
    lane = lax.broadcasted_iota(jnp.int32, (capacity, tokens.shape[0]), 1)
    chosen = jnp.where(lane == index[:, :1], 1.0, 0.0).astype(jnp.bfloat16)
    x[...] = half(product(chosen, tokens_here[...]))
    e[...] = half(scale[:, :1] * grad_here[...].astype(jnp.float32))
    rows[0] = x[...]
    rows[1] = e[...]


def pick(tokens, slot_token, slot_count, slot_gate, grad_out):
    capacity, width = grad_out.shape
    inputs = (slot_token, slot_count, slot_gate, tokens, grad_out)
    return pl.pallas_call(
        pick_kernel,
        out_shape=(
            held((2, capacity, width)),
            held((capacity, width)),
            held((capacity, width)),
            held((capacity, 128), jnp.float32),
            TURN,
        ),
        in_specs=[SMEM] + [HBM] * 5,
        out_specs=(VMEM,) * 5,
        scratch_shapes=[pltpu.SMEM(v.shape, v.dtype) for v in inputs[:3]]
        + [pltpu.VMEM(v.shape, v.dtype) for v in inputs[3:]]
        + [pltpu.SemaphoreType.DMA((5,))],
        compiler_params=limit(4),
        cost_estimate=cost(0, 0),
        name="pick",
    )(lax.axis_index("dp")[None], *(in_hbm(v) for v in inputs))


def last_split_kernel(level, x_far, e_far, w_gate, w_up, w_down, _, x, e, panels, turn, arrived):
    loads = [
        pltpu.make_async_copy(w, panels.at[i], arrived.at[i])
        for i, w in enumerate((w_gate, w_up, w_down))
    ]
    for copy in loads:
        copy.start()
    split_body(level, x, e)
    turn[...] = jnp.zeros_like(turn)
    for copy in loads:
        copy.wait()


def last_split(level, fars, weights, turn):
    rows = held(level.shape[1:])
    return pl.pallas_call(
        last_split_kernel,
        out_shape=(rows, rows, held((3, *weights[0].shape)), TURN),
        in_specs=[VMEM] * 3 + [HBM] * 3 + [VMEM],
        out_specs=(VMEM,) * 4,
        scratch_shapes=[pltpu.SemaphoreType.DMA((3,))],
        compiler_params=limit(4),
        cost_estimate=cost(0, 0),
        name="split_2",
    )(*fetched(level, *fars), *(in_hbm(w) for w in weights), *fetched(turn))


def expert_kernel(count, *refs):
    parts, refs = refs[: 4 * count], refs[4 * count :]
    near, other, _, x, e, hidden, gate_grad, up_grad, out_keep, out_send, row_keep, row_send, turn = refs
    turn[...] = jnp.zeros_like(turn)
    units = near.shape[1]
    rows = x.shape[0] // 4
    size = rows // count
    for i in range(count):
        x_pair, x_far, e_pair, e_far = parts[4 * i : 4 * i + 4]
        for plane, (x_from, e_from, x_half, e_half) in enumerate(
            ((x_pair, e_pair, 0, 0), (x_pair, e_far, 1, 0), (x_far, e_pair, 0, 1), (x_far, e_far, 1, 1))
        ):
            into = slice(plane * rows + i * size, plane * rows + (i + 1) * size)
            x[into] = x_from[x_half * size : (x_half + 1) * size]
            e[into] = e_from[e_half * size : (e_half + 1) * size]
    for i, panels in enumerate((near, other)):
        mine = slice(i * units, (i + 1) * units)
        gate_pre = row_product(x[...], panels[0])
        up_pre = row_product(x[...], panels[1])
        hidden_grad = row_product(e[...], panels[2])
        gate_sig = jax.nn.sigmoid(gate_pre)
        activated = gate_pre * gate_sig
        hidden[:, mine] = half(activated * up_pre)
        gate_grad[:, mine] = half(
            hidden_grad * up_pre * (gate_sig * (1.0 + gate_pre * (1.0 - gate_sig)))
        )
        up_grad[:, mine] = half(hidden_grad * activated)
    for at in range(0, x.shape[1], PANEL):
        part = slice(at, at + PANEL)
        out = product(hidden[:, :units], near[2, :, part]) + product(
            hidden[:, units:], other[2, :, part]
        )
        out_keep[:, part] = out[: 2 * rows]
        out_send[:, part] = half(out[2 * rows :])
        row = (
            product(gate_grad[:, :units], near[0, :, part])
            + product(gate_grad[:, units:], other[0, :, part])
            + product(up_grad[:, :units], near[1, :, part])
            + product(up_grad[:, units:], other[1, :, part])
        )
        row_keep[:rows, part] = row[:rows]
        row_keep[rows:, part] = row[2 * rows : 3 * rows]
        row_send[:rows, part] = half(row[rows : 2 * rows])
        row_send[rows:, part] = half(row[3 * rows :])


def expert(parts, near, other, turn):
    rows, width = 2 * sum(part[0].shape[0] for part in parts), parts[0][0].shape[1]
    units = 2 * near.shape[1]
    saved, kept, sent = (
        held((rows, units)),
        held((rows // 2, width), jnp.float32),
        held((rows // 2, width)),
    )
    return pl.pallas_call(
        functools.partial(expert_kernel, len(parts)),
        out_shape=(held((rows, width)),) * 2 + (saved,) * 3 + (kept, sent, kept, sent, TURN),
        in_specs=[VMEM] * (4 * len(parts) + 3),
        out_specs=(VMEM,) * 10,
        compiler_params=limit(12),
        cost_estimate=cost(12 * rows * units * width, 6 * units * width),
        name="expert",
    )(*fetched(*(ref for part in parts for ref in part), near, other, turn))


def slot_sums(works, units, columns):
    x, e, hidden, gate_grad, up_grad = (
        [refs[i][:, units if i > 1 else columns] for refs in works] for i in range(5)
    )
    for left, right in ((gate_grad, x), (up_grad, x), (hidden, e)):
        yield col_product(jnp.concatenate(left, 0), jnp.concatenate(right, 0))


def other_kernel(*refs):
    works, (_, grads, turn) = (refs[:5], refs[5:10]), refs[10:]
    turn[...] = jnp.zeros_like(turn)
    units = grads.shape[1]
    for at in range(0, grads.shape[2], PANEL):
        columns = slice(at, at + PANEL)
        for i, total in enumerate(slot_sums(works, slice(units, 2 * units), columns)):
            grads[i, :, columns] = half(total)


def other_grads(works, turn):
    width = works[0][0].shape[1]
    units = works[0][2].shape[1] // 2
    return pl.pallas_call(
        other_kernel,
        out_shape=(held((3, units, width)), TURN),
        in_specs=[VMEM] * 11,
        out_specs=(VMEM, VMEM),
        compiler_params=limit(8),
        cost_estimate=cost(LONG, 0),
        name="other_grads",
    )(*fetched(*works[0], *works[1], turn))


def own_kernel(factor, *refs):
    works, (received, _, *grads, turn) = (refs[:5], refs[5:10]), refs[10:]
    turn[...] = jnp.zeros_like(turn)
    units = received.shape[1]
    columns = pl.ds(pl.multiple_of(pl.program_id(0) * PANEL, PANEL), PANEL)
    for i, total in enumerate(slot_sums(works, slice(0, units), columns)):
        total = total + received[i, :, columns].astype(jnp.float32)
        grads[i][...] = (total * factor).astype(grads[i].dtype)


def own_grads(works, received, turn, factor, dtype):
    _, units, width = received.shape
    block = pl.BlockSpec((units, PANEL), lambda i: (0, i))
    return pl.pallas_call(
        functools.partial(own_kernel, factor),
        grid=(width // PANEL,),
        out_shape=(shape((units, width), dtype),) * 3 + (TURN,),
        in_specs=[VMEM] * 12,
        out_specs=(block,) * 3 + (VMEM,),
        compiler_params=limit(12),
        cost_estimate=cost(0, 0),
        name="own_grads",
    )(*fetched(*works[0], *works[1], received, turn))


def staged(body, name, outs, *values, flops=0):
    def kernel(*refs):
        refs[-1][...] = jnp.zeros(TURN.shape, TURN.dtype)
        body(*refs[: len(values) - 1], *refs[len(values) : -1])

    return pl.pallas_call(
        kernel,
        out_shape=(*outs, TURN),
        in_specs=[VMEM] * len(values),
        out_specs=(VMEM,) * (len(outs) + 1),
        compiler_params=limit(4),
        cost_estimate=cost(flops, 0),
        name=name,
    )(*fetched(*values))


def split_body(*refs):
    levels, (x, e) = refs[:-2], refs[-2:]
    rows = levels[0].shape[1]
    for i, level in enumerate(levels):
        x[i * rows : (i + 1) * rows] = level[0]
        e[i * rows : (i + 1) * rows] = level[1]


def pair_body(x, x_side, e, e_side, x_pair, e_pair):
    rows = x.shape[0]
    for out, near, side in ((x_pair, x, x_side), (e_pair, e, e_side)):
        out[:rows] = near[...]
        out[rows:] = side[...]


def plane_body(out_keep, out_far, row_keep, row_far, out_mid, out_side, row_mid, row_side):
    rows = out_mid.shape[0]
    for keep, far, mid, side in (
        (out_keep, out_far, out_mid, out_side),
        (row_keep, row_far, row_mid, row_side),
    ):
        mid[...] = keep[:rows] + far[:rows].astype(jnp.float32)
        side[...] = half(keep[rows:] + far[rows:].astype(jnp.float32))


def line_body(out_mid, out_side, row_mid, row_side, first, second):
    rows = first.shape[1]
    for i, (mid, side) in enumerate(((out_mid, out_side), (row_mid, row_side))):
        total = mid[...] + side[...].astype(jnp.float32)
        first[i] = total[:rows].astype(first.dtype)
        second[i] = total[rows:].astype(second.dtype)


def far_body(own, one, three, total):
    total[...] = own[...] + one[...].astype(jnp.float32) + three[...].astype(jnp.float32)


def final_body(total, two, weight, expert_out, grad_rows):
    expert_out[...] = half(weight[:, :1] * (total[0] + two[0].astype(jnp.float32)))
    grad_rows[...] = half(total[1] + two[1].astype(jnp.float32))


def shards(tokens, slot_token, slot_count, slot_gate, grad_out, w_gate, w_up, w_down):
    capacity = slot_gate.shape[0]
    devices = lax.axis_size("dp")
    all_bits = devices.bit_length() - 1
    core, along_x, along_y = 1 << CORE, 1 << LINK_X, 1 << LINK_Y
    far_bits = range(ROW_BITS + 1, all_bits)

    weights = [w_gate, w_up, w_down]
    for bit in far_bits:
        weights = [jnp.concatenate([w, swapped(w, 1 << bit)], 0) for w in weights]
    own, x, e, weight, turn = pick(tokens, slot_token, slot_count, slot_gate, grad_out)

    width = own.shape[2]
    rows = 2 * capacity

    def sides_of(x, e):
        return x, swapped(x, along_x), e, swapped(e, along_y)

    def fars_of(x, e):
        return x, swapped(x, along_y), e, swapped(e, along_x)

    one, three, two = (swapped(own, k << LINK_Z) for k in (1, 3, 2))
    x, e, turn = staged(pair_body, "pair_0", [held((rows, width))] * 2, *sides_of(x, e), turn)
    part_0 = fars_of(x, e)
    x, e, turn = staged(split_body, "split_13", [held((rows, width))] * 2, one, three, turn)
    sides_13 = sides_of(x, e)
    x, e, near, turn = last_split(two, part_0[1::2], weights, turn)
    sides_2 = sides_of(x, e)
    other = swapped(near, core)
    x, e, turn = staged(pair_body, "pair_13", [held((2 * rows, width))] * 2, *sides_13, turn)
    part_13 = fars_of(x, e)
    x, e, turn = staged(pair_body, "pair_2", [held((rows, width))] * 2, *sides_2, turn, flops=LONG)
    part_2 = fars_of(x, e)

    works, sides = [], []
    for parts in ((part_13,), (part_0, part_2)):
        *work, out_keep, out_send, row_keep, row_send, turn = expert(parts, near, other, turn)
        works.append(work)
        sides.append((out_keep, swapped(out_send, along_y), row_keep, swapped(row_send, along_x)))

    whole, piece = held((rows, width), jnp.float32), held((rows, width))

    def plane_sum(side, turn):
        out_mid, out_side, row_mid, row_side, turn = staged(
            plane_body, "plane_sum", [whole, piece, whole, piece], *side, turn
        )
        return (out_mid, swapped(out_side, along_x), row_mid, swapped(row_side, along_y)), turn

    def line_sum(middle, turn, first, flops=0):
        level_dims = (2, capacity, width)
        return staged(
            line_body, "line_sum", [held(level_dims, first), held(level_dims)], *middle, turn,
            flops=flops,
        )

    middle_13, turn = plane_sum(sides[0], turn)
    sent, turn = other_grads(works, turn)
    received = swapped(sent, core)
    middle_02, turn = plane_sum(sides[1], turn)
    sum_1, sum_3, turn = line_sum(middle_13, turn, jnp.bfloat16)
    one, three = swapped(sum_1, 1 << LINK_Z), swapped(sum_3, 3 << LINK_Z)
    sum_0, sum_2, turn = line_sum(middle_02, turn, jnp.float32, flops=LONG)
    two = swapped(sum_2, 2 << LINK_Z)
    factor = 1.0 / math.sqrt(devices * capacity)
    if far_bits:
        *owned, turn = own_grads(works, received, turn, 1.0, jnp.float32)
        for bit in reversed(far_bits):
            cut = owned[0].shape[0] // 2
            owned = [t[:cut] + swapped(half(t[cut:]), 1 << bit) for t in owned]
        owned = [half(total * factor) for total in owned]
    else:
        *owned, turn = own_grads(works, received, turn, factor, jnp.bfloat16)
    total, turn = staged(
        far_body, "far_sum", [held(own.shape, jnp.float32)], sum_0, one, three, turn, flops=LONG // 10
    )
    expert_out, grad_rows, turn = staged(
        final_body, "final", [shape((capacity, width))] * 2, total, two, weight, turn
    )
    return (expert_out, grad_rows, *owned)


def solution(mesh):
    return jax.shard_map(
        shards,
        mesh=mesh,
        in_specs=(
            P("dp", None),
            P("dp"),
            P(),
            P("dp"),
            P("dp", None),
            P("dp", None),
            P("dp", None),
            P("dp", None),
        ),
        out_specs=(P("dp", None), P("dp", None), P("dp", None), P("dp", None), P("dp", None)),
        check_vma=False,
    )
```

```python
import functools
import math

import jax
import jax.numpy as jnp
from jax import lax
from jax.experimental import pallas as pl
from jax.experimental.pallas import tpu as pltpu
from jax.sharding import PartitionSpec as P

CORE, LINK_X, LINK_Y, LINK_Z = 0, 1, 2, 3
ROW_BITS = 4
LONG = 10**11
C_PACK = 0
C_PAIR3 = 0
C_SPLIT3 = LONG * 4 // 100
C_SPLIT2 = LONG * 3 // 100
C_PAIR2 = LONG // 100
C_COPY = 0
PANEL = 512
TURN = pltpu.VMEM((8, 128), jnp.float32)
VMEM = pl.BlockSpec(memory_space=pltpu.VMEM)
HBM = pl.BlockSpec(memory_space=pltpu.HBM)
SMEM = pl.BlockSpec(memory_space=pltpu.SMEM)


def swapped(block, mask):
    count = lax.axis_size("dp")
    return lax.ppermute(block, "dp", [(low, low ^ mask) for low in range(count)])


def row_product(left, right):
    return lax.dot_general(
        left, right, (((1,), (1,)), ((), ())), preferred_element_type=jnp.float32
    )


def col_product(left, right):
    return lax.dot_general(
        left, right, (((0,), (0,)), ((), ())), preferred_element_type=jnp.float32
    )


def product(left, right):
    return jnp.dot(left, right, preferred_element_type=jnp.float32)


def half(value):
    return value.astype(jnp.bfloat16)


def shape(dims, dtype=jnp.bfloat16):
    return jax.ShapeDtypeStruct(dims, dtype)


def held(dims, dtype=jnp.bfloat16):
    return pltpu.VMEM(dims, dtype)


def fetched(*values):
    return [pltpu.with_memory_space_constraint(value, pltpu.VMEM) for value in values]


def in_hbm(value):
    return pltpu.with_memory_space_constraint(value, pltpu.HBM)


def limit(mib):
    return pltpu.CompilerParams(vmem_limit_bytes=mib << 20)


def cost(flops, moved):
    return pl.CostEstimate(flops=flops, bytes_accessed=moved, transcendentals=0)


def pick_kernel(
    place, token, count, gate, tokens, grad, w_gate, w_up, w_down, rows, weight, panels, turn,
    token_here, count_here, gate_here, tokens_here, grad_here, arrived,
):
    pairs = (
        (token, token_here),
        (count, count_here),
        (gate, gate_here),
        (tokens, tokens_here),
        (grad, grad_here),
    )
    copies = [pltpu.make_async_copy(*pair, arrived.at[i]) for i, pair in enumerate(pairs)]
    loads = [
        pltpu.make_async_copy(w, panels.at[i], arrived.at[len(pairs) + i])
        for i, w in enumerate((w_gate, w_up, w_down))
    ]
    for copy in copies + loads:
        copy.start()
    turn[...] = jnp.zeros_like(turn)
    for copy in copies:
        copy.wait()
    capacity, lanes = weight.shape
    row = lax.broadcasted_iota(jnp.int32, (capacity, lanes), 0)
    live = count_here[place[0]]
    index = jnp.zeros((capacity, lanes), jnp.int32)
    scale = jnp.zeros((capacity, lanes), jnp.float32)
    for slot in range(capacity):
        index = jnp.where(row == slot, token_here[slot], index)
        scale = jnp.where(row == slot, jnp.where(slot < live, gate_here[slot], 0.0), scale)
    weight[...] = scale
    lane = lax.broadcasted_iota(jnp.int32, (capacity, tokens.shape[0]), 1)
    chosen = jnp.where(lane == index[:, :1], 1.0, 0.0).astype(jnp.bfloat16)
    rows[0] = half(product(chosen, tokens_here[...]))
    rows[1] = half(scale[:, :1] * grad_here[...].astype(jnp.float32))
    for copy in loads:
        copy.wait()


def pick(tokens, slot_token, slot_count, slot_gate, grad_out, weights):
    capacity, width = grad_out.shape
    inputs = (slot_token, slot_count, slot_gate, tokens, grad_out)
    return pl.pallas_call(
        pick_kernel,
        out_shape=(
            held((2, capacity, width)),
            held((capacity, 128), jnp.float32),
            held((3, *weights[0].shape)),
            TURN,
        ),
        in_specs=[SMEM] + [HBM] * 8,
        out_specs=(VMEM,) * 4,
        scratch_shapes=[pltpu.SMEM(v.shape, v.dtype) for v in inputs[:3]]
        + [pltpu.VMEM(v.shape, v.dtype) for v in inputs[3:]]
        + [pltpu.SemaphoreType.DMA((8,))],
        compiler_params=limit(4),
        cost_estimate=cost(0, 0),
        name="pick",
    )(lax.axis_index("dp")[None], *(in_hbm(v) for v in (*inputs, *weights)))


def expert_kernel(sizes, *refs):
    parts = []
    for size in sizes:
        part, refs = refs[:size], refs[size:]
        if size == 1:
            cut = part[0].shape[0] // 4
            part = [part[0].at[i * cut : (i + 1) * cut] for i in range(4)]
        parts.append(part)
    near, other, _, x, e, hidden, gate_grad, up_grad, out_keep, out_send, row_keep, row_send, turn = refs
    turn[...] = jnp.zeros_like(turn)
    units = near.shape[1]
    rows = x.shape[0] // 4
    size = rows // len(parts)
    for i, (x_pair, x_far, e_pair, e_far) in enumerate(parts):
        for plane, (x_from, e_from, x_half, e_half) in enumerate(
            ((x_pair, e_pair, 0, 0), (x_pair, e_far, 1, 0), (x_far, e_pair, 0, 1), (x_far, e_far, 1, 1))
        ):
            into = slice(plane * rows + i * size, plane * rows + (i + 1) * size)
            x[into] = x_from[x_half * size : (x_half + 1) * size]
            e[into] = e_from[e_half * size : (e_half + 1) * size]
    for i, panels in enumerate((near, other)):
        mine = slice(i * units, (i + 1) * units)
        gate_pre = row_product(panels[0], x[...])
        up_pre = row_product(panels[1], x[...])
        hidden_grad = row_product(panels[2], e[...])
        gate_sig = jax.nn.sigmoid(gate_pre)
        activated = gate_pre * gate_sig
        hidden[mine] = half(activated * up_pre)
        gate_grad[mine] = half(
            hidden_grad * up_pre * (gate_sig * (1.0 + gate_pre * (1.0 - gate_sig)))
        )
        up_grad[mine] = half(hidden_grad * activated)
    for at in range(0, x.shape[1], PANEL):
        part = slice(at, at + PANEL)
        out = col_product(hidden[:units], near[2, :, part]) + col_product(
            hidden[units:], other[2, :, part]
        )
        out_keep[:, part] = out[: 2 * rows]
        out_send[:, part] = half(out[2 * rows :])
        row = (
            col_product(gate_grad[:units], near[0, :, part])
            + col_product(gate_grad[units:], other[0, :, part])
            + col_product(up_grad[:units], near[1, :, part])
            + col_product(up_grad[units:], other[1, :, part])
        )
        row_keep[:rows, part] = row[:rows]
        row_keep[rows:, part] = row[2 * rows : 3 * rows]
        row_send[:rows, part] = half(row[rows : 2 * rows])
        row_send[rows:, part] = half(row[3 * rows :])


def expert(parts, near, other, turn):
    rows = sum(ref.shape[0] for part in parts for ref in part) // 2
    width = parts[0][0].shape[1]
    units = 2 * near.shape[1]
    saved, kept, sent = (
        held((units, rows)),
        held((rows // 2, width), jnp.float32),
        held((rows // 2, width)),
    )
    return pl.pallas_call(
        functools.partial(expert_kernel, [len(part) for part in parts]),
        out_shape=(held((rows, width)),) * 2 + (saved,) * 3 + (kept, sent, kept, sent, TURN),
        in_specs=[VMEM] * (sum(len(part) for part in parts) + 3),
        out_specs=(VMEM,) * 10,
        compiler_params=limit(12),
        cost_estimate=cost(12 * rows * units * width, 6 * units * width),
        name="expert",
    )(*fetched(*(ref for part in parts for ref in part), near, other, turn))


def slot_sums(works, units, columns):
    x, e = (jnp.concatenate([refs[i][:, columns] for refs in works], 0) for i in (0, 1))
    for i, right in ((3, x), (4, x), (2, e)):
        yield product(jnp.concatenate([refs[i][units] for refs in works], 1), right)


def other_kernel(*refs):
    works, (_, grads, turn) = (refs[:5], refs[5:10]), refs[10:]
    turn[...] = jnp.zeros_like(turn)
    units = grads.shape[1]
    for at in range(0, grads.shape[2], PANEL):
        columns = slice(at, at + PANEL)
        for i, total in enumerate(slot_sums(works, slice(units, 2 * units), columns)):
            grads[i, :, columns] = half(total)


def other_grads(works, turn):
    width = works[0][0].shape[1]
    units = works[0][2].shape[0] // 2
    return pl.pallas_call(
        other_kernel,
        out_shape=(held((3, units, width)), TURN),
        in_specs=[VMEM] * 11,
        out_specs=(VMEM, VMEM),
        compiler_params=limit(8),
        cost_estimate=cost(LONG // 50, 0),
        name="other_grads",
    )(*fetched(*works[0], *works[1], turn))


def own_kernel(factor, *refs):
    works, (received, _, *grads, turn) = (refs[:5], refs[5:10]), refs[10:]
    turn[...] = jnp.zeros_like(turn)
    units = received.shape[1]
    columns = pl.ds(pl.multiple_of(pl.program_id(0) * PANEL, PANEL), PANEL)
    for i, total in enumerate(slot_sums(works, slice(0, units), columns)):
        total = total + received[i, :, columns].astype(jnp.float32)
        grads[i][...] = (total * factor).astype(grads[i].dtype)


def own_grads(works, received, turn, factor, dtype):
    _, units, width = received.shape
    block = pl.BlockSpec((units, PANEL), lambda i: (0, i))
    return pl.pallas_call(
        functools.partial(own_kernel, factor),
        grid=(width // PANEL,),
        out_shape=(shape((units, width), dtype),) * 3 + (TURN,),
        in_specs=[VMEM] * 12,
        out_specs=(block,) * 3 + (VMEM,),
        compiler_params=limit(12),
        cost_estimate=cost(0, 0),
        name="own_grads",
    )(*fetched(*works[0], *works[1], received, turn))


def staged(body, name, outs, *values, flops=0):
    def kernel(*refs):
        refs[-1][...] = jnp.zeros(TURN.shape, TURN.dtype)
        body(*refs[: len(values) - 1], *refs[len(values) : -1])

    return pl.pallas_call(
        kernel,
        out_shape=(*outs, TURN),
        in_specs=[VMEM] * len(values),
        out_specs=(VMEM,) * (len(outs) + 1),
        compiler_params=limit(4),
        cost_estimate=cost(flops, 0),
        name=name,
    )(*fetched(*values))


def split_body(*refs):
    levels, (x, e) = refs[:-2], refs[-2:]
    rows = levels[0].shape[1]
    for i, level in enumerate(levels):
        x[i * rows : (i + 1) * rows] = level[0]
        e[i * rows : (i + 1) * rows] = level[1]


def pair_body(x, x_side, e, e_side, x_pair, e_pair):
    rows = x.shape[0]
    for out, near, side in ((x_pair, x, x_side), (e_pair, e, e_side)):
        out[:rows] = near[...]
        out[rows:] = side[...]


def first_pair_body(x, x_side, e, e_side, _, x_pair, e_pair):
    pair_body(x, x_side, e, e_side, x_pair, e_pair)


def pack_body(x_pair, x_far, e_pair, e_far, plane):
    rows = x_pair.shape[0]
    for i, part in enumerate((x_pair, x_far, e_pair, e_far)):
        plane[i * rows : (i + 1) * rows] = part[...]


def copy_body(rows, again, x, e):
    again[...] = rows[...]
    x[...] = rows[0]
    e[...] = rows[1]


def plane_body(out_keep, out_far, row_keep, row_far, out_mid, out_side, row_mid, row_side):
    rows = out_mid.shape[0]
    for keep, far, mid, side in (
        (out_keep, out_far, out_mid, out_side),
        (row_keep, row_far, row_mid, row_side),
    ):
        mid[...] = keep[:rows] + far[:rows].astype(jnp.float32)
        side[...] = half(keep[rows:] + far[rows:].astype(jnp.float32))


def line_body(out_mid, out_side, row_mid, row_side, first, second):
    rows = first.shape[1]
    for i, (mid, side) in enumerate(((out_mid, out_side), (row_mid, row_side))):
        total = mid[...] + side[...].astype(jnp.float32)
        first[i] = total[:rows].astype(first.dtype)
        second[i] = total[rows:].astype(second.dtype)


def far_body(own, three, total):
    total[...] = own[...] + three[...].astype(jnp.float32)


def final_body(total, one, two, weight, expert_out, grad_rows):
    out, row = (
        total[i] + one[i].astype(jnp.float32) + two[i].astype(jnp.float32) for i in (0, 1)
    )
    expert_out[...] = half(weight[:, :1] * out)
    grad_rows[...] = half(row)


def shards(tokens, slot_token, slot_count, slot_gate, grad_out, w_gate, w_up, w_down):
    capacity = slot_gate.shape[0]
    devices = lax.axis_size("dp")
    all_bits = devices.bit_length() - 1
    core, along_x, along_y = 1 << CORE, 1 << LINK_X, 1 << LINK_Y
    far_bits = range(ROW_BITS + 1, all_bits)

    weights = [w_gate, w_up, w_down]
    for bit in far_bits:
        weights = [jnp.concatenate([w, swapped(w, 1 << bit)], 0) for w in weights]
    own, weight, near, turn = pick(
        tokens, slot_token, slot_count, slot_gate, grad_out, weights
    )
    other = swapped(near, core)

    width = own.shape[2]
    rows = 2 * capacity

    def sides_of(x, e):
        return x, swapped(x, along_x), e, swapped(e, along_y)

    def fars_of(x, e):
        return x, swapped(x, along_y), e, swapped(e, along_x)

    three = swapped(own, 3 << LINK_Z)
    one_level, two_levels = [held((capacity, width))] * 2, [held((rows, width))] * 2
    own, x, e, turn = staged(
        copy_body, "copy", [held(own.shape), *one_level], own, turn, flops=C_COPY
    )
    two = swapped(own, 2 << LINK_Z)
    x, e, turn = staged(first_pair_body, "pair_0", two_levels, *sides_of(x, e), other, turn)
    part_0 = fars_of(x, e)
    x, e, turn = staged(split_body, "split_3", one_level, three, turn, flops=C_SPLIT3)
    sides_3 = sides_of(x, e)
    plane, turn = staged(pack_body, "pack", [held((4 * rows, width))], *part_0, turn, flops=C_PACK)
    part_1 = (swapped(plane, 1 << LINK_Z),)
    x, e, turn = staged(pair_body, "pair_3", two_levels, *sides_3, turn, flops=C_PAIR3)
    part_3 = fars_of(x, e)
    x, e, turn = staged(split_body, "split_2", one_level, two, turn, flops=C_SPLIT2)
    sides_2 = sides_of(x, e)
    x, e, turn = staged(pair_body, "pair_2", two_levels, *sides_2, turn, flops=C_PAIR2)
    part_2 = fars_of(x, e)

    works, sides = [], []
    for parts in ((part_0, part_3), (part_1, part_2)):
        *work, out_keep, out_send, row_keep, row_send, turn = expert(parts, near, other, turn)
        works.append(work)
        sides.append((out_keep, swapped(out_send, along_y), row_keep, swapped(row_send, along_x)))

    whole, piece = held((rows, width), jnp.float32), held((rows, width))

    def plane_sum(side, turn):
        out_mid, out_side, row_mid, row_side, turn = staged(
            plane_body, "plane_sum", [whole, piece, whole, piece], *side, turn
        )
        return (out_mid, swapped(out_side, along_x), row_mid, swapped(row_side, along_y)), turn

    def line_sum(middle, turn, first, flops=0):
        level_dims = (2, capacity, width)
        return staged(
            line_body, "line_sum", [held(level_dims, first), held(level_dims)], *middle, turn,
            flops=flops,
        )

    middle_03, turn = plane_sum(sides[0], turn)
    sent, turn = other_grads(works, turn)
    received = swapped(sent, core)
    middle_12, turn = plane_sum(sides[1], turn)
    sum_0, sum_3, turn = line_sum(middle_03, turn, jnp.float32)
    three = swapped(sum_3, 3 << LINK_Z)
    sum_1, sum_2, turn = line_sum(middle_12, turn, jnp.bfloat16, flops=LONG)
    two, one = swapped(sum_2, 2 << LINK_Z), swapped(sum_1, 1 << LINK_Z)
    factor = 1.0 / math.sqrt(devices * capacity)
    if far_bits:
        *owned, turn = own_grads(works, received, turn, 1.0, jnp.float32)
        for bit in reversed(far_bits):
            cut = owned[0].shape[0] // 2
            owned = [t[:cut] + swapped(half(t[cut:]), 1 << bit) for t in owned]
        owned = [half(total * factor) for total in owned]
    else:
        *owned, turn = own_grads(works, received, turn, factor, jnp.bfloat16)
    total, turn = staged(
        far_body, "far_sum", [held(own.shape, jnp.float32)], sum_0, three, turn, flops=LONG // 10
    )
    expert_out, grad_rows, turn = staged(
        final_body, "final", [shape((capacity, width))] * 2, total, one, two, weight, turn
    )
    return (expert_out, grad_rows, *owned)


def solution(mesh):
    return jax.shard_map(
        shards,
        mesh=mesh,
        in_specs=(
            P("dp", None),
            P("dp"),
            P(),
            P("dp"),
            P("dp", None),
            P("dp", None),
            P("dp", None),
            P("dp", None),
        ),
        out_specs=(P("dp", None), P("dp", None), P("dp", None), P("dp", None), P("dp", None)),
        check_vma=False,
    )
```

```python
import functools
import math

import jax
import jax.numpy as jnp
from jax import lax
from jax.experimental import pallas as pl
from jax.experimental.pallas import tpu as pltpu
from jax.sharding import PartitionSpec as P

CORE, LINK_X, LINK_Y, LINK_Z = 0, 1, 2, 3
ROW_BITS = 4
LONG = 10**11
C_PACK = 0
C_PAIR_FIRST = 0
C_FIRST = LONG * 4 // 100
C_LAST = LONG * 3 // 100
C_PAIR_LAST = LONG // 100
C_COPY = 0
C_TURN = 0
PANEL = 512
TURN = pltpu.VMEM((8, 128), jnp.float32)
VMEM = pl.BlockSpec(memory_space=pltpu.VMEM)
HBM = pl.BlockSpec(memory_space=pltpu.HBM)
SMEM = pl.BlockSpec(memory_space=pltpu.SMEM)


def swapped(block, mask):
    count = lax.axis_size("dp")
    return lax.ppermute(block, "dp", [(low, low ^ mask) for low in range(count)])


def shifted(block, steps):
    count = lax.axis_size("dp")
    span = 1 << (ROW_BITS + 1)
    rise = (steps << LINK_Z) % span
    route = [(low, low // span * span + (low + rise) % span) for low in range(count)]
    return lax.ppermute(block, "dp", route)


def row_product(left, right):
    return lax.dot_general(
        left, right, (((1,), (1,)), ((), ())), preferred_element_type=jnp.float32
    )


def col_product(left, right):
    return lax.dot_general(
        left, right, (((0,), (0,)), ((), ())), preferred_element_type=jnp.float32
    )


def product(left, right):
    return jnp.dot(left, right, preferred_element_type=jnp.float32)


def half(value):
    return value.astype(jnp.bfloat16)


def shape(dims, dtype=jnp.bfloat16):
    return jax.ShapeDtypeStruct(dims, dtype)


def held(dims, dtype=jnp.bfloat16):
    return pltpu.VMEM(dims, dtype)


def fetched(*values):
    return [pltpu.with_memory_space_constraint(value, pltpu.VMEM) for value in values]


def in_hbm(value):
    return pltpu.with_memory_space_constraint(value, pltpu.HBM)


def limit(mib):
    return pltpu.CompilerParams(vmem_limit_bytes=mib << 20)


def cost(flops, moved):
    return pl.CostEstimate(flops=flops, bytes_accessed=moved, transcendentals=0)


def pick_kernel(
    place, token, count, gate, tokens, grad, w_gate, w_up, w_down, rows, weight, panels, turn,
    token_here, count_here, gate_here, tokens_here, grad_here, arrived,
):
    pairs = (
        (token, token_here),
        (count, count_here),
        (gate, gate_here),
        (tokens, tokens_here),
        (grad, grad_here),
    )
    copies = [pltpu.make_async_copy(*pair, arrived.at[i]) for i, pair in enumerate(pairs)]
    loads = [
        pltpu.make_async_copy(w, panels.at[i], arrived.at[len(pairs) + i])
        for i, w in enumerate((w_gate, w_up, w_down))
    ]
    for copy in copies + loads:
        copy.start()
    turn[...] = jnp.zeros_like(turn)
    for copy in copies:
        copy.wait()
    capacity, lanes = weight.shape
    row = lax.broadcasted_iota(jnp.int32, (capacity, lanes), 0)
    live = count_here[place[0]]
    index = jnp.zeros((capacity, lanes), jnp.int32)
    scale = jnp.zeros((capacity, lanes), jnp.float32)
    for slot in range(capacity):
        index = jnp.where(row == slot, token_here[slot], index)
        scale = jnp.where(row == slot, jnp.where(slot < live, gate_here[slot], 0.0), scale)
    weight[...] = scale
    lane = lax.broadcasted_iota(jnp.int32, (capacity, tokens.shape[0]), 1)
    chosen = jnp.where(lane == index[:, :1], 1.0, 0.0).astype(jnp.bfloat16)
    rows[0] = half(product(chosen, tokens_here[...]))
    rows[1] = half(scale[:, :1] * grad_here[...].astype(jnp.float32))
    for copy in loads:
        copy.wait()


def pick(tokens, slot_token, slot_count, slot_gate, grad_out, weights):
    capacity, width = grad_out.shape
    inputs = (slot_token, slot_count, slot_gate, tokens, grad_out)
    return pl.pallas_call(
        pick_kernel,
        out_shape=(
            held((2, capacity, width)),
            held((capacity, 128), jnp.float32),
            held((3, *weights[0].shape)),
            TURN,
        ),
        in_specs=[SMEM] + [HBM] * 8,
        out_specs=(VMEM,) * 4,
        scratch_shapes=[pltpu.SMEM(v.shape, v.dtype) for v in inputs[:3]]
        + [pltpu.VMEM(v.shape, v.dtype) for v in inputs[3:]]
        + [pltpu.SemaphoreType.DMA((8,))],
        compiler_params=limit(4),
        cost_estimate=cost(0, 0),
        name="pick",
    )(lax.axis_index("dp")[None], *(in_hbm(v) for v in (*inputs, *weights)))


def expert_kernel(sizes, *refs):
    parts = []
    for size in sizes:
        part, refs = refs[:size], refs[size:]
        if size == 1:
            cut = part[0].shape[0] // 4
            part = [part[0].at[i * cut : (i + 1) * cut] for i in range(4)]
        parts.append(part)
    near, other, near_turned, other_turned, _, *refs = refs
    x, e, hidden, gate_grad, up_grad, out_keep, out_send, row_keep, row_send, turn = refs
    turn[...] = jnp.zeros_like(turn)
    units = near.shape[1]
    rows = x.shape[0] // 4
    size = rows // len(parts)
    for i, (x_pair, x_far, e_pair, e_far) in enumerate(parts):
        for plane, (x_from, e_from, x_half, e_half) in enumerate(
            ((x_pair, e_pair, 0, 0), (x_pair, e_far, 1, 0), (x_far, e_pair, 0, 1), (x_far, e_far, 1, 1))
        ):
            into = slice(plane * rows + i * size, plane * rows + (i + 1) * size)
            x[into] = x_from[x_half * size : (x_half + 1) * size]
            e[into] = e_from[e_half * size : (e_half + 1) * size]
    for i, panels in enumerate((near_turned, other_turned)):
        mine = slice(i * units, (i + 1) * units)
        gate_pre = product(x[...], panels[0])
        up_pre = product(x[...], panels[1])
        hidden_grad = product(e[...], panels[2])
        gate_sig = jax.nn.sigmoid(gate_pre)
        activated = gate_pre * gate_sig
        hidden[:, mine] = half(activated * up_pre)
        gate_grad[:, mine] = half(
            hidden_grad * up_pre * (gate_sig * (1.0 + gate_pre * (1.0 - gate_sig)))
        )
        up_grad[:, mine] = half(hidden_grad * activated)
    for at in range(0, x.shape[1], PANEL):
        part = slice(at, at + PANEL)
        out = product(hidden[:, :units], near[2, :, part]) + product(
            hidden[:, units:], other[2, :, part]
        )
        out_keep[:, part] = out[: 2 * rows]
        out_send[:, part] = half(out[2 * rows :])
        row = (
            product(gate_grad[:, :units], near[0, :, part])
            + product(gate_grad[:, units:], other[0, :, part])
            + product(up_grad[:, :units], near[1, :, part])
            + product(up_grad[:, units:], other[1, :, part])
        )
        row_keep[:rows, part] = row[:rows]
        row_keep[rows:, part] = row[2 * rows : 3 * rows]
        row_send[:rows, part] = half(row[rows : 2 * rows])
        row_send[rows:, part] = half(row[3 * rows :])


def expert(parts, panels, turn):
    rows = sum(ref.shape[0] for part in parts for ref in part) // 2
    width = parts[0][0].shape[1]
    units = 2 * panels[0].shape[1]
    saved, kept, sent = (
        held((rows, units)),
        held((rows // 2, width), jnp.float32),
        held((rows // 2, width)),
    )
    return pl.pallas_call(
        functools.partial(expert_kernel, [len(part) for part in parts]),
        out_shape=(held((rows, width)),) * 2 + (saved,) * 3 + (kept, sent, kept, sent, TURN),
        in_specs=[VMEM] * (sum(len(part) for part in parts) + 5),
        out_specs=(VMEM,) * 10,
        compiler_params=limit(12),
        cost_estimate=cost(12 * rows * units * width, 6 * units * width),
        name="expert",
    )(*fetched(*(ref for part in parts for ref in part), *panels, turn))


def slot_sums(works, units, columns):
    x, e, hidden, gate_grad, up_grad = (
        jnp.concatenate([refs[i][:, units if i > 1 else columns] for refs in works], 0)
        for i in range(5)
    )
    for left, right in ((gate_grad, x), (up_grad, x), (hidden, e)):
        yield col_product(left, right)


def other_kernel(*refs):
    works, (_, grads, turn) = (refs[:5], refs[5:10]), refs[10:]
    turn[...] = jnp.zeros_like(turn)
    units = grads.shape[1]
    for at in range(0, grads.shape[2], PANEL):
        columns = slice(at, at + PANEL)
        for i, total in enumerate(slot_sums(works, slice(units, 2 * units), columns)):
            grads[i, :, columns] = half(total)


def other_grads(works, turn):
    width = works[0][0].shape[1]
    units = works[0][2].shape[1] // 2
    return pl.pallas_call(
        other_kernel,
        out_shape=(held((3, units, width)), TURN),
        in_specs=[VMEM] * 11,
        out_specs=(VMEM, VMEM),
        compiler_params=limit(8),
        cost_estimate=cost(LONG // 50, 0),
        name="other_grads",
    )(*fetched(*works[0], *works[1], turn))


def own_kernel(factor, *refs):
    works, (received, _, *grads, turn) = (refs[:5], refs[5:10]), refs[10:]
    turn[...] = jnp.zeros_like(turn)
    units = received.shape[1]
    columns = pl.ds(pl.multiple_of(pl.program_id(0) * PANEL, PANEL), PANEL)
    for i, total in enumerate(slot_sums(works, slice(0, units), columns)):
        total = total + received[i, :, columns].astype(jnp.float32)
        grads[i][...] = (total * factor).astype(grads[i].dtype)


def own_grads(works, received, turn, factor, dtype):
    _, units, width = received.shape
    block = pl.BlockSpec((units, PANEL), lambda i: (0, i))
    return pl.pallas_call(
        functools.partial(own_kernel, factor),
        grid=(width // PANEL,),
        out_shape=(shape((units, width), dtype),) * 3 + (TURN,),
        in_specs=[VMEM] * 12,
        out_specs=(block,) * 3 + (VMEM,),
        compiler_params=limit(12),
        cost_estimate=cost(0, 0),
        name="own_grads",
    )(*fetched(*works[0], *works[1], received, turn))


def staged(body, name, outs, *values, flops=0):
    def kernel(*refs):
        refs[-1][...] = jnp.zeros(TURN.shape, TURN.dtype)
        body(*refs[: len(values) - 1], *refs[len(values) : -1])

    return pl.pallas_call(
        kernel,
        out_shape=(*outs, TURN),
        in_specs=[VMEM] * len(values),
        out_specs=(VMEM,) * (len(outs) + 1),
        compiler_params=limit(4),
        cost_estimate=cost(flops, 0),
        name=name,
    )(*fetched(*values))


def split_body(*refs):
    levels, (x, e) = refs[:-2], refs[-2:]
    rows = levels[0].shape[1]
    for i, level in enumerate(levels):
        x[i * rows : (i + 1) * rows] = level[0]
        e[i * rows : (i + 1) * rows] = level[1]


def pair_body(x, x_side, e, e_side, x_pair, e_pair):
    rows = x.shape[0]
    for out, near, side in ((x_pair, x, x_side), (e_pair, e, e_side)):
        out[:rows] = near[...]
        out[rows:] = side[...]


def first_pair_body(x, x_side, e, e_side, _, x_pair, e_pair):
    pair_body(x, x_side, e, e_side, x_pair, e_pair)


def turn_body(panels, turned):
    for i in range(panels.shape[0]):
        for at in range(0, panels.shape[2], PANEL):
            turned[i, at : at + PANEL] = panels[i, :, at : at + PANEL].T


def pack_body(x_pair, x_far, e_pair, e_far, plane):
    rows = x_pair.shape[0]
    for i, part in enumerate((x_pair, x_far, e_pair, e_far)):
        plane[i * rows : (i + 1) * rows] = part[...]


def copy_body(rows, again, x, e):
    again[...] = rows[...]
    x[...] = rows[0]
    e[...] = rows[1]


def plane_body(out_keep, out_far, row_keep, row_far, out_mid, out_side, row_mid, row_side):
    rows = out_mid.shape[0]
    for keep, far, mid, side in (
        (out_keep, out_far, out_mid, out_side),
        (row_keep, row_far, row_mid, row_side),
    ):
        mid[...] = keep[:rows] + far[:rows].astype(jnp.float32)
        side[...] = half(keep[rows:] + far[rows:].astype(jnp.float32))


def line_body(out_mid, out_side, row_mid, row_side, first, second):
    rows = first.shape[1]
    for i, (mid, side) in enumerate(((out_mid, out_side), (row_mid, row_side))):
        total = mid[...] + side[...].astype(jnp.float32)
        first[i] = total[:rows].astype(first.dtype)
        second[i] = total[rows:].astype(second.dtype)


def relay_body(own, passed, total):
    total[...] = half(own[...] + passed[...].astype(jnp.float32))


def near_body(own, three, total):
    total[...] = own[...] + three[...].astype(jnp.float32)


def final_body(total, one, weight, expert_out, grad_rows):
    out, row = (total[i] + one[i].astype(jnp.float32) for i in (0, 1))
    expert_out[...] = half(weight[:, :1] * out)
    grad_rows[...] = half(row)


def shards(tokens, slot_token, slot_count, slot_gate, grad_out, w_gate, w_up, w_down):
    capacity = slot_gate.shape[0]
    devices = lax.axis_size("dp")
    all_bits = devices.bit_length() - 1
    core, along_x, along_y = 1 << CORE, 1 << LINK_X, 1 << LINK_Y
    far_bits = range(ROW_BITS + 1, all_bits)

    weights = [w_gate, w_up, w_down]
    for bit in far_bits:
        weights = [jnp.concatenate([w, swapped(w, 1 << bit)], 0) for w in weights]
    own, weight, near, turn = pick(
        tokens, slot_token, slot_count, slot_gate, grad_out, weights
    )
    other = swapped(near, core)

    width = own.shape[2]
    rows = 2 * capacity

    def sides_of(x, e):
        return x, swapped(x, along_x), e, swapped(e, along_y)

    def fars_of(x, e):
        return x, swapped(x, along_y), e, swapped(e, along_x)

    two = shifted(own, 2)
    one_level, two_levels = [held((capacity, width))] * 2, [held((rows, width))] * 2
    own, x, e, turn = staged(
        copy_body, "copy", [held(own.shape), *one_level], own, turn, flops=C_COPY
    )
    one = shifted(own, 1)
    turned = held((near.shape[0], near.shape[2], near.shape[1]))
    near_turned, turn = staged(turn_body, "turn_near", [turned], near, turn, flops=C_TURN)
    x, e, turn = staged(first_pair_body, "pair_0", two_levels, *sides_of(x, e), other, turn)
    part_0 = fars_of(x, e)
    x, e, turn = staged(split_body, "split_2", one_level, two, turn, flops=C_FIRST)
    sides_2 = sides_of(x, e)
    plane, turn = staged(pack_body, "pack", [held((4 * rows, width))], *part_0, turn, flops=C_PACK)
    part_3 = (shifted(plane, -1),)
    x, e, turn = staged(pair_body, "pair_2", two_levels, *sides_2, turn, flops=C_PAIR_FIRST)
    part_2 = fars_of(x, e)
    x, e, turn = staged(split_body, "split_1", one_level, one, turn, flops=C_LAST)
    sides_1 = sides_of(x, e)
    other_turned, turn = staged(turn_body, "turn_other", [turned], other, turn, flops=C_TURN)
    panels = (near, other, near_turned, other_turned)
    x, e, turn = staged(pair_body, "pair_1", two_levels, *sides_1, turn, flops=C_PAIR_LAST)
    part_1 = fars_of(x, e)

    works, sides = [], []
    for parts in ((part_0, part_2), (part_1, part_3)):
        *work, out_keep, out_send, row_keep, row_send, turn = expert(parts, panels, turn)
        works.append(work)
        sides.append((out_keep, swapped(out_send, along_y), row_keep, swapped(row_send, along_x)))

    whole, piece = held((rows, width), jnp.float32), held((rows, width))

    def plane_sum(side, turn):
        out_mid, out_side, row_mid, row_side, turn = staged(
            plane_body, "plane_sum", [whole, piece, whole, piece], *side, turn
        )
        return (out_mid, swapped(out_side, along_x), row_mid, swapped(row_side, along_y)), turn

    def line_sum(middle, turn, first, flops=0):
        level_dims = (2, capacity, width)
        return staged(
            line_body, "line_sum", [held(level_dims, first), held(level_dims)], *middle, turn,
            flops=flops,
        )

    middle_02, turn = plane_sum(sides[0], turn)
    sent, turn = other_grads(works, turn)
    received = swapped(sent, core)
    middle_31, turn = plane_sum(sides[1], turn)
    sum_0, sum_2, turn = line_sum(middle_02, turn, jnp.float32)
    passed = shifted(sum_2, -1)
    sum_1, sum_3, turn = line_sum(middle_31, turn, jnp.float32)
    three = shifted(sum_3, 1)
    sum_1, turn = staged(relay_body, "relay", [held(own.shape)], sum_1, passed, turn, flops=LONG)
    one = shifted(sum_1, -1)
    factor = 1.0 / math.sqrt(devices * capacity)
    if far_bits:
        *owned, turn = own_grads(works, received, turn, 1.0, jnp.float32)
        for bit in reversed(far_bits):
            cut = owned[0].shape[0] // 2
            owned = [t[:cut] + swapped(half(t[cut:]), 1 << bit) for t in owned]
        owned = [half(total * factor) for total in owned]
    else:
        *owned, turn = own_grads(works, received, turn, factor, jnp.bfloat16)
    total, turn = staged(
        near_body, "near_sum", [held(own.shape, jnp.float32)], sum_0, three, turn, flops=LONG // 10
    )
    expert_out, grad_rows, turn = staged(
        final_body, "final", [shape((capacity, width))] * 2, total, one, weight, turn
    )
    return (expert_out, grad_rows, *owned)


def solution(mesh):
    return jax.shard_map(
        shards,
        mesh=mesh,
        in_specs=(
            P("dp", None),
            P("dp"),
            P(),
            P("dp"),
            P("dp", None),
            P("dp", None),
            P("dp", None),
            P("dp", None),
        ),
        out_specs=(P("dp", None), P("dp", None), P("dp", None), P("dp", None), P("dp", None)),
        check_vma=False,
    )
```

```python
import functools
import math

import jax
import jax.numpy as jnp
from jax import lax
from jax.experimental import pallas as pl
from jax.experimental.pallas import tpu as pltpu
from jax.sharding import PartitionSpec as P

CORE, LINK_X, LINK_Y, LINK_Z = 0, 1, 2, 3
ROW_BITS = 4
LONG = 10**11
C_PACK = 0
C_PAIR_FIRST = 0
C_FIRST = LONG * 4 // 100
C_LAST = LONG * 3 // 100
C_PAIR_LAST = LONG // 100
C_COPY = LONG // 5
C_TURN = 0
C_LOAD = LONG // 5
PANEL = 512
TURN = pltpu.VMEM((8, 128), jnp.float32)
VMEM = pl.BlockSpec(memory_space=pltpu.VMEM)
HBM = pl.BlockSpec(memory_space=pltpu.HBM)
SMEM = pl.BlockSpec(memory_space=pltpu.SMEM)


def swapped(block, mask):
    count = lax.axis_size("dp")
    return lax.ppermute(block, "dp", [(low, low ^ mask) for low in range(count)])


def shifted(block, steps):
    count = lax.axis_size("dp")
    span = 1 << (ROW_BITS + 1)
    rise = (steps << LINK_Z) % span
    route = [(low, low // span * span + (low + rise) % span) for low in range(count)]
    return lax.ppermute(block, "dp", route)


def row_product(left, right):
    return lax.dot_general(
        left, right, (((1,), (1,)), ((), ())), preferred_element_type=jnp.float32
    )


def col_product(left, right):
    return lax.dot_general(
        left, right, (((0,), (0,)), ((), ())), preferred_element_type=jnp.float32
    )


def product(left, right):
    return jnp.dot(left, right, preferred_element_type=jnp.float32)


def half(value):
    return value.astype(jnp.bfloat16)


def shape(dims, dtype=jnp.bfloat16):
    return jax.ShapeDtypeStruct(dims, dtype)


def held(dims, dtype=jnp.bfloat16):
    return pltpu.VMEM(dims, dtype)


def fetched(*values):
    return [pltpu.with_memory_space_constraint(value, pltpu.VMEM) for value in values]


def in_hbm(value):
    return pltpu.with_memory_space_constraint(value, pltpu.HBM)


def limit(mib):
    return pltpu.CompilerParams(vmem_limit_bytes=mib << 20)


def cost(flops, moved):
    return pl.CostEstimate(flops=flops, bytes_accessed=moved, transcendentals=0)


def pick_kernel(
    place, token, count, gate, tokens, grad, rows, weight, turn,
    token_here, count_here, gate_here, tokens_here, grad_here, arrived,
):
    pairs = (
        (token, token_here),
        (count, count_here),
        (gate, gate_here),
        (tokens, tokens_here),
        (grad, grad_here),
    )
    copies = [pltpu.make_async_copy(*pair, arrived.at[i]) for i, pair in enumerate(pairs)]
    for copy in copies:
        copy.start()
    turn[...] = jnp.zeros_like(turn)
    for copy in copies:
        copy.wait()
    capacity, lanes = weight.shape
    row = lax.broadcasted_iota(jnp.int32, (capacity, lanes), 0)
    live = count_here[place[0]]
    index = jnp.zeros((capacity, lanes), jnp.int32)
    scale = jnp.zeros((capacity, lanes), jnp.float32)
    for slot in range(capacity):
        index = jnp.where(row == slot, token_here[slot], index)
        scale = jnp.where(row == slot, jnp.where(slot < live, gate_here[slot], 0.0), scale)
    weight[...] = scale
    lane = lax.broadcasted_iota(jnp.int32, (capacity, tokens.shape[0]), 1)
    chosen = jnp.where(lane == index[:, :1], 1.0, 0.0).astype(jnp.bfloat16)
    rows[0] = half(product(chosen, tokens_here[...]))
    rows[1] = half(scale[:, :1] * grad_here[...].astype(jnp.float32))


def pick(tokens, slot_token, slot_count, slot_gate, grad_out):
    capacity, width = grad_out.shape
    inputs = (slot_token, slot_count, slot_gate, tokens, grad_out)
    return pl.pallas_call(
        pick_kernel,
        out_shape=(
            held((2, capacity, width)),
            held((capacity, 128), jnp.float32),
            TURN,
        ),
        in_specs=[SMEM] + [HBM] * 5,
        out_specs=(VMEM,) * 3,
        scratch_shapes=[pltpu.SMEM(v.shape, v.dtype) for v in inputs[:3]]
        + [pltpu.VMEM(v.shape, v.dtype) for v in inputs[3:]]
        + [pltpu.SemaphoreType.DMA((5,))],
        compiler_params=limit(4),
        cost_estimate=cost(0, 0),
        name="pick",
    )(lax.axis_index("dp")[None], *(in_hbm(v) for v in inputs))


def expert_kernel(sizes, *refs):
    parts = []
    for size in sizes:
        part, refs = refs[:size], refs[size:]
        if size == 1:
            cut = part[0].shape[0] // 4
            part = [part[0].at[i * cut : (i + 1) * cut] for i in range(4)]
        parts.append(part)
    near, other, (near_turned, other_turned, _) = refs[:3], refs[3:6], refs[6:9]
    refs = refs[9:]
    x, e, hidden, gate_grad, up_grad, out_keep, out_send, row_keep, row_send, turn = refs
    turn[...] = jnp.zeros_like(turn)
    units = near[0].shape[0]
    rows = x.shape[0] // 4
    size = rows // len(parts)
    for i, (x_pair, x_far, e_pair, e_far) in enumerate(parts):
        for plane, (x_from, e_from, x_half, e_half) in enumerate(
            ((x_pair, e_pair, 0, 0), (x_pair, e_far, 1, 0), (x_far, e_pair, 0, 1), (x_far, e_far, 1, 1))
        ):
            into = slice(plane * rows + i * size, plane * rows + (i + 1) * size)
            x[into] = x_from[x_half * size : (x_half + 1) * size]
            e[into] = e_from[e_half * size : (e_half + 1) * size]
    for i, panels in enumerate((near_turned, other_turned)):
        mine = slice(i * units, (i + 1) * units)
        gate_pre = product(x[...], panels[0])
        up_pre = product(x[...], panels[1])
        hidden_grad = product(e[...], panels[2])
        gate_sig = jax.nn.sigmoid(gate_pre)
        activated = gate_pre * gate_sig
        hidden[:, mine] = half(activated * up_pre)
        gate_grad[:, mine] = half(
            hidden_grad * up_pre * (gate_sig * (1.0 + gate_pre * (1.0 - gate_sig)))
        )
        up_grad[:, mine] = half(hidden_grad * activated)
    for at in range(0, x.shape[1], PANEL):
        part = slice(at, at + PANEL)
        out = product(hidden[:, :units], near[2][:, part]) + product(
            hidden[:, units:], other[2][:, part]
        )
        out_keep[:, part] = out[: 2 * rows]
        out_send[:, part] = half(out[2 * rows :])
        row = (
            product(gate_grad[:, :units], near[0][:, part])
            + product(gate_grad[:, units:], other[0][:, part])
            + product(up_grad[:, :units], near[1][:, part])
            + product(up_grad[:, units:], other[1][:, part])
        )
        row_keep[:rows, part] = row[:rows]
        row_keep[rows:, part] = row[2 * rows : 3 * rows]
        row_send[:rows, part] = half(row[rows : 2 * rows])
        row_send[rows:, part] = half(row[3 * rows :])


def expert(parts, panels, turn):
    rows = sum(ref.shape[0] for part in parts for ref in part) // 2
    width = parts[0][0].shape[1]
    units = 2 * panels[0].shape[0]
    saved, kept, sent = (
        held((rows, units)),
        held((rows // 2, width), jnp.float32),
        held((rows // 2, width)),
    )
    return pl.pallas_call(
        functools.partial(expert_kernel, [len(part) for part in parts]),
        out_shape=(held((rows, width)),) * 2 + (saved,) * 3 + (kept, sent, kept, sent, TURN),
        in_specs=[VMEM] * (sum(len(part) for part in parts) + 9),
        out_specs=(VMEM,) * 10,
        compiler_params=limit(12),
        cost_estimate=cost(12 * rows * units * width, 6 * units * width),
        name="expert",
    )(*fetched(*(ref for part in parts for ref in part), *panels, turn))


def slot_sums(works, units, columns):
    x, e, hidden, gate_grad, up_grad = (
        jnp.concatenate([refs[i][:, units if i > 1 else columns] for refs in works], 0)
        for i in range(5)
    )
    for left, right in ((gate_grad, x), (up_grad, x), (hidden, e)):
        yield col_product(left, right)


def other_kernel(*refs):
    works, (_, grads, turn) = (refs[:5], refs[5:10]), refs[10:]
    turn[...] = jnp.zeros_like(turn)
    units = grads.shape[1]
    for at in range(0, grads.shape[2], PANEL):
        columns = slice(at, at + PANEL)
        for i, total in enumerate(slot_sums(works, slice(units, 2 * units), columns)):
            grads[i, :, columns] = half(total)


def other_grads(works, turn):
    width = works[0][0].shape[1]
    units = works[0][2].shape[1] // 2
    return pl.pallas_call(
        other_kernel,
        out_shape=(held((3, units, width)), TURN),
        in_specs=[VMEM] * 11,
        out_specs=(VMEM, VMEM),
        compiler_params=limit(8),
        cost_estimate=cost(LONG // 50, 0),
        name="other_grads",
    )(*fetched(*works[0], *works[1], turn))


def own_kernel(factor, *refs):
    works, (received, _, *grads, turn) = (refs[:5], refs[5:10]), refs[10:]
    turn[...] = jnp.zeros_like(turn)
    units = received.shape[1]
    columns = pl.ds(pl.multiple_of(pl.program_id(0) * PANEL, PANEL), PANEL)
    for i, total in enumerate(slot_sums(works, slice(0, units), columns)):
        total = total + received[i, :, columns].astype(jnp.float32)
        grads[i][...] = (total * factor).astype(grads[i].dtype)


def own_grads(works, received, turn, factor, dtype):
    _, units, width = received.shape
    block = pl.BlockSpec((units, PANEL), lambda i: (0, i))
    return pl.pallas_call(
        functools.partial(own_kernel, factor),
        grid=(width // PANEL,),
        out_shape=(shape((units, width), dtype),) * 3 + (TURN,),
        in_specs=[VMEM] * 12,
        out_specs=(block,) * 3 + (VMEM,),
        compiler_params=limit(12),
        cost_estimate=cost(0, 0),
        name="own_grads",
    )(*fetched(*works[0], *works[1], received, turn))


def staged(body, name, outs, *values, flops=0):
    def kernel(*refs):
        refs[-1][...] = jnp.zeros(TURN.shape, TURN.dtype)
        body(*refs[: len(values) - 1], *refs[len(values) : -1])

    return pl.pallas_call(
        kernel,
        out_shape=(*outs, TURN),
        in_specs=[VMEM] * len(values),
        out_specs=(VMEM,) * (len(outs) + 1),
        compiler_params=limit(4),
        cost_estimate=cost(flops, 0),
        name=name,
    )(*fetched(*values))


def split_body(*refs):
    levels, (x, e) = refs[:-2], refs[-2:]
    rows = levels[0].shape[1]
    for i, level in enumerate(levels):
        x[i * rows : (i + 1) * rows] = level[0]
        e[i * rows : (i + 1) * rows] = level[1]


def pair_body(x, x_side, e, e_side, x_pair, e_pair):
    rows = x.shape[0]
    for out, near, side in ((x_pair, x, x_side), (e_pair, e, e_side)):
        out[:rows] = near[...]
        out[rows:] = side[...]


def first_pair_body(x, x_side, e, e_side, up, down, x_pair, e_pair, rows):
    pair_body(x, x_side, e, e_side, x_pair, e_pair)
    rows[0] = x[...]
    rows[1] = e[...]


def turn_body(*refs):
    near, other, turned = refs[:3], refs[3:6], refs[6:]
    for panels, into in zip((near, other), turned):
        for i, panel in enumerate(panels):
            for at in range(0, panel.shape[1], PANEL):
                into[i, at : at + PANEL] = panel[:, at : at + PANEL].T


def pack_body(x_pair, x_far, e_pair, e_far, plane):
    rows = x_pair.shape[0]
    for i, part in enumerate((x_pair, x_far, e_pair, e_far)):
        plane[i * rows : (i + 1) * rows] = part[...]


def spread_body(rows, gate, x, e):
    x[...] = rows[0]
    e[...] = rows[1]


def plane_body(out_keep, out_far, row_keep, row_far, out_mid, out_side, row_mid, row_side):
    rows = out_mid.shape[0]
    for keep, far, mid, side in (
        (out_keep, out_far, out_mid, out_side),
        (row_keep, row_far, row_mid, row_side),
    ):
        mid[...] = keep[:rows] + far[:rows].astype(jnp.float32)
        side[...] = half(keep[rows:] + far[rows:].astype(jnp.float32))


def line_body(out_mid, out_side, row_mid, row_side, first, second):
    rows = first.shape[1]
    for i, (mid, side) in enumerate(((out_mid, out_side), (row_mid, row_side))):
        total = mid[...] + side[...].astype(jnp.float32)
        first[i] = total[:rows].astype(first.dtype)
        second[i] = total[rows:].astype(second.dtype)


def relay_body(own, passed, total):
    total[...] = half(own[...] + passed[...].astype(jnp.float32))


def near_body(own, three, total):
    total[...] = own[...] + three[...].astype(jnp.float32)


def final_body(total, one, weight, expert_out, grad_rows):
    out, row = (total[i] + one[i].astype(jnp.float32) for i in (0, 1))
    expert_out[...] = half(weight[:, :1] * out)
    grad_rows[...] = half(row)


def shards(tokens, slot_token, slot_count, slot_gate, grad_out, w_gate, w_up, w_down):
    capacity = slot_gate.shape[0]
    devices = lax.axis_size("dp")
    all_bits = devices.bit_length() - 1
    core, along_x, along_y = 1 << CORE, 1 << LINK_X, 1 << LINK_Y
    far_bits = range(ROW_BITS + 1, all_bits)

    weights = [w_gate, w_up, w_down]
    for bit in far_bits:
        weights = [jnp.concatenate([w, swapped(w, 1 << bit)], 0) for w in weights]
    own, weight, turn = pick(tokens, slot_token, slot_count, slot_gate, grad_out)
    other = [swapped(w, core) for w in weights]

    width = own.shape[2]
    rows = 2 * capacity

    def sides_of(x, e):
        return x, swapped(x, along_x), e, swapped(e, along_y)

    def fars_of(x, e):
        return x, swapped(x, along_y), e, swapped(e, along_x)

    two = shifted(own, 2)
    one_level, two_levels = [held((capacity, width))] * 2, [held((rows, width))] * 2
    x, e, turn = staged(spread_body, "spread", one_level, own, other[0], turn, flops=C_COPY)
    x, e, own, turn = staged(
        first_pair_body, "pair_0", [*two_levels, held(own.shape)], *sides_of(x, e), *other[1:], turn
    )
    one = shifted(own, 1)
    part_0 = fars_of(x, e)
    x, e, turn = staged(split_body, "split_2", one_level, two, turn, flops=C_FIRST)
    sides_2 = sides_of(x, e)
    plane, turn = staged(pack_body, "pack", [held((4 * rows, width))], *part_0, turn, flops=C_PACK)
    part_3 = (shifted(plane, -1),)
    x, e, turn = staged(pair_body, "pair_2", two_levels, *sides_2, turn, flops=C_PAIR_FIRST)
    part_2 = fars_of(x, e)
    x, e, turn = staged(split_body, "split_1", one_level, one, turn, flops=C_LAST)
    sides_1 = sides_of(x, e)
    turned = held((3, *weights[0].shape[::-1]))
    near_turned, other_turned, turn = staged(
        turn_body, "turn_panels", [turned] * 2, *weights, *other, turn, flops=C_TURN
    )
    panels = (*weights, *other, near_turned, other_turned)
    x, e, turn = staged(pair_body, "pair_1", two_levels, *sides_1, turn, flops=C_PAIR_LAST)
    part_1 = fars_of(x, e)

    works, sides = [], []
    for parts in ((part_0, part_2), (part_1, part_3)):
        *work, out_keep, out_send, row_keep, row_send, turn = expert(parts, panels, turn)
        works.append(work)
        sides.append((out_keep, swapped(out_send, along_y), row_keep, swapped(row_send, along_x)))

    whole, piece = held((rows, width), jnp.float32), held((rows, width))

    def plane_sum(side, turn):
        out_mid, out_side, row_mid, row_side, turn = staged(
            plane_body, "plane_sum", [whole, piece, whole, piece], *side, turn
        )
        return (out_mid, swapped(out_side, along_x), row_mid, swapped(row_side, along_y)), turn

    def line_sum(middle, turn, first, flops=0):
        level_dims = (2, capacity, width)
        return staged(
            line_body, "line_sum", [held(level_dims, first), held(level_dims)], *middle, turn,
            flops=flops,
        )

    middle_02, turn = plane_sum(sides[0], turn)
    sent, turn = other_grads(works, turn)
    received = swapped(sent, core)
    middle_31, turn = plane_sum(sides[1], turn)
    sum_0, sum_2, turn = line_sum(middle_02, turn, jnp.float32)
    passed = shifted(sum_2, -1)
    sum_1, sum_3, turn = line_sum(middle_31, turn, jnp.float32)
    three = shifted(sum_3, 1)
    sum_1, turn = staged(relay_body, "relay", [held(own.shape)], sum_1, passed, turn, flops=LONG)
    one = shifted(sum_1, -1)
    factor = 1.0 / math.sqrt(devices * capacity)
    if far_bits:
        *owned, turn = own_grads(works, received, turn, 1.0, jnp.float32)
        for bit in reversed(far_bits):
            cut = owned[0].shape[0] // 2
            owned = [t[:cut] + swapped(half(t[cut:]), 1 << bit) for t in owned]
        owned = [half(total * factor) for total in owned]
    else:
        *owned, turn = own_grads(works, received, turn, factor, jnp.bfloat16)
    total, turn = staged(
        near_body, "near_sum", [held(own.shape, jnp.float32)], sum_0, three, turn, flops=LONG // 10
    )
    expert_out, grad_rows, turn = staged(
        final_body, "final", [shape((capacity, width))] * 2, total, one, weight, turn
    )
    return (expert_out, grad_rows, *owned)


def solution(mesh):
    return jax.shard_map(
        shards,
        mesh=mesh,
        in_specs=(
            P("dp", None),
            P("dp"),
            P(),
            P("dp"),
            P("dp", None),
            P("dp", None),
            P("dp", None),
            P("dp", None),
        ),
        out_specs=(P("dp", None), P("dp", None), P("dp", None), P("dp", None), P("dp", None)),
        check_vma=False,
    )
```

```python
import functools
import math

import jax
import jax.numpy as jnp
from jax import lax
from jax.experimental import pallas as pl
from jax.experimental.pallas import tpu as pltpu
from jax.sharding import PartitionSpec as P

CORE, LINK_X, LINK_Y, LINK_Z = 0, 1, 2, 3
ROW_BITS = 4
LONG = 10**11
C_PACK = 0
C_PAIR_FIRST = 0
C_FIRST = LONG * 4 // 100
C_LAST = LONG * 3 // 100
C_PAIR_LAST = LONG // 100
C_COPY = LONG // 5
C_TURN = 0
C_LOAD = LONG // 5
PANEL = 512
WIDE = 1536
TURN = pltpu.VMEM((8, 128), jnp.float32)
VMEM = pl.BlockSpec(memory_space=pltpu.VMEM)
HBM = pl.BlockSpec(memory_space=pltpu.HBM)
SMEM = pl.BlockSpec(memory_space=pltpu.SMEM)


def swapped(block, mask):
    count = lax.axis_size("dp")
    return lax.ppermute(block, "dp", [(low, low ^ mask) for low in range(count)])


def shifted(block, steps):
    count = lax.axis_size("dp")
    span = 1 << (ROW_BITS + 1)
    rise = (steps << LINK_Z) % span
    route = [(low, low // span * span + (low + rise) % span) for low in range(count)]
    return lax.ppermute(block, "dp", route)


def row_product(left, right):
    return lax.dot_general(
        left, right, (((1,), (1,)), ((), ())), preferred_element_type=jnp.float32
    )


def col_product(left, right):
    return lax.dot_general(
        left, right, (((0,), (0,)), ((), ())), preferred_element_type=jnp.float32
    )


def product(left, right):
    return jnp.dot(left, right, preferred_element_type=jnp.float32)


def half(value):
    return value.astype(jnp.bfloat16)


def shape(dims, dtype=jnp.bfloat16):
    return jax.ShapeDtypeStruct(dims, dtype)


def held(dims, dtype=jnp.bfloat16):
    return pltpu.VMEM(dims, dtype)


def fetched(*values):
    return [pltpu.with_memory_space_constraint(value, pltpu.VMEM) for value in values]


def in_hbm(value):
    return pltpu.with_memory_space_constraint(value, pltpu.HBM)


def limit(mib):
    return pltpu.CompilerParams(vmem_limit_bytes=mib << 20)


def cost(flops, moved):
    return pl.CostEstimate(flops=flops, bytes_accessed=moved, transcendentals=0)


def pick_kernel(
    place, token, count, gate, tokens, grad, rows, weight, turn,
    token_here, count_here, gate_here, tokens_here, grad_here, arrived,
):
    pairs = (
        (token, token_here),
        (count, count_here),
        (gate, gate_here),
        (tokens, tokens_here),
        (grad, grad_here),
    )
    copies = [pltpu.make_async_copy(*pair, arrived.at[i]) for i, pair in enumerate(pairs)]
    for copy in copies:
        copy.start()
    turn[...] = jnp.zeros_like(turn)
    for copy in copies:
        copy.wait()
    capacity, lanes = weight.shape
    row = lax.broadcasted_iota(jnp.int32, (capacity, lanes), 0)
    live = count_here[place[0]]
    index = jnp.zeros((capacity, lanes), jnp.int32)
    scale = jnp.zeros((capacity, lanes), jnp.float32)
    for slot in range(capacity):
        index = jnp.where(row == slot, token_here[slot], index)
        scale = jnp.where(row == slot, jnp.where(slot < live, gate_here[slot], 0.0), scale)
    weight[...] = scale
    lane = lax.broadcasted_iota(jnp.int32, (capacity, tokens.shape[0]), 1)
    chosen = jnp.where(lane == index[:, :1], 1.0, 0.0).astype(jnp.bfloat16)
    rows[0] = half(product(chosen, tokens_here[...]))
    rows[1] = half(scale[:, :1] * grad_here[...].astype(jnp.float32))


def pick(tokens, slot_token, slot_count, slot_gate, grad_out):
    capacity, width = grad_out.shape
    inputs = (slot_token, slot_count, slot_gate, tokens, grad_out)
    return pl.pallas_call(
        pick_kernel,
        out_shape=(
            held((2, capacity, width)),
            held((capacity, 128), jnp.float32),
            TURN,
        ),
        in_specs=[SMEM] + [HBM] * 5,
        out_specs=(VMEM,) * 3,
        scratch_shapes=[pltpu.SMEM(v.shape, v.dtype) for v in inputs[:3]]
        + [pltpu.VMEM(v.shape, v.dtype) for v in inputs[3:]]
        + [pltpu.SemaphoreType.DMA((5,))],
        compiler_params=limit(4),
        cost_estimate=cost(0, 0),
        name="pick",
    )(lax.axis_index("dp")[None], *(in_hbm(v) for v in inputs))


def expert_kernel(sizes, *refs):
    parts = []
    for size in sizes:
        part, refs = refs[:size], refs[size:]
        if size == 1:
            cut = part[0].shape[0] // 4
            part = [part[0].at[i * cut : (i + 1) * cut] for i in range(4)]
        parts.append(part)
    near, other, (near_turned, other_turned, _) = refs[:3], refs[3:6], refs[6:9]
    refs = refs[9:]
    x, e, hidden, gate_grad, up_grad, out_keep, out_send, row_keep, row_send, turn = refs
    turn[...] = jnp.zeros_like(turn)
    units = near[0].shape[0]
    rows = x.shape[0] // 4
    size = rows // len(parts)
    for i, (x_pair, x_far, e_pair, e_far) in enumerate(parts):
        for plane, (x_from, e_from, x_half, e_half) in enumerate(
            ((x_pair, e_pair, 0, 0), (x_pair, e_far, 1, 0), (x_far, e_pair, 0, 1), (x_far, e_far, 1, 1))
        ):
            into = slice(plane * rows + i * size, plane * rows + (i + 1) * size)
            x[into] = x_from[x_half * size : (x_half + 1) * size]
            e[into] = e_from[e_half * size : (e_half + 1) * size]
    for i, panels in enumerate((near_turned, other_turned)):
        mine = slice(i * units, (i + 1) * units)
        gate_pre = product(x[...], panels[0])
        up_pre = product(x[...], panels[1])
        hidden_grad = product(e[...], panels[2])
        gate_sig = jax.nn.sigmoid(gate_pre)
        activated = gate_pre * gate_sig
        hidden[:, mine] = half(activated * up_pre)
        gate_grad[:, mine] = half(
            hidden_grad * up_pre * (gate_sig * (1.0 + gate_pre * (1.0 - gate_sig)))
        )
        up_grad[:, mine] = half(hidden_grad * activated)
    for at in range(0, x.shape[1], PANEL):
        part = slice(at, at + PANEL)
        out = product(hidden[:, :units], near[2][:, part]) + product(
            hidden[:, units:], other[2][:, part]
        )
        out_keep[:, part] = out[: 2 * rows]
        out_send[:, part] = half(out[2 * rows :])
        row = (
            product(gate_grad[:, :units], near[0][:, part])
            + product(gate_grad[:, units:], other[0][:, part])
            + product(up_grad[:, :units], near[1][:, part])
            + product(up_grad[:, units:], other[1][:, part])
        )
        row_keep[:rows, part] = row[:rows]
        row_keep[rows:, part] = row[2 * rows : 3 * rows]
        row_send[:rows, part] = half(row[rows : 2 * rows])
        row_send[rows:, part] = half(row[3 * rows :])


def expert(parts, panels, turn):
    rows = sum(ref.shape[0] for part in parts for ref in part) // 2
    width = parts[0][0].shape[1]
    units = 2 * panels[0].shape[0]
    saved, kept, sent = (
        held((rows, units)),
        held((rows // 2, width), jnp.float32),
        held((rows // 2, width)),
    )
    return pl.pallas_call(
        functools.partial(expert_kernel, [len(part) for part in parts]),
        out_shape=(held((rows, width)),) * 2 + (saved,) * 3 + (kept, sent, kept, sent, TURN),
        in_specs=[VMEM] * (sum(len(part) for part in parts) + 9),
        out_specs=(VMEM,) * 10,
        compiler_params=limit(12),
        cost_estimate=cost(12 * rows * units * width, 6 * units * width),
        name="expert",
    )(*fetched(*(ref for part in parts for ref in part), *panels, turn))


def slot_sums(works, units, columns):
    x, e, hidden, gate_grad, up_grad = (
        jnp.concatenate([refs[i][:, units if i > 1 else columns] for refs in works], 0)
        for i in range(5)
    )
    for left, right in ((gate_grad, x), (up_grad, x), (hidden, e)):
        yield col_product(left, right)


def other_kernel(*refs):
    works, (_, grads, turn) = (refs[:5], refs[5:10]), refs[10:]
    turn[...] = jnp.zeros_like(turn)
    units = grads.shape[1]
    for at in range(0, grads.shape[2], PANEL):
        columns = slice(at, at + PANEL)
        for i, total in enumerate(slot_sums(works, slice(units, 2 * units), columns)):
            grads[i, :, columns] = half(total)


def other_grads(works, turn):
    width = works[0][0].shape[1]
    units = works[0][2].shape[1] // 2
    return pl.pallas_call(
        other_kernel,
        out_shape=(held((3, units, width)), TURN),
        in_specs=[VMEM] * 11,
        out_specs=(VMEM, VMEM),
        compiler_params=limit(8),
        cost_estimate=cost(LONG // 50, 0),
        name="other_grads",
    )(*fetched(*works[0], *works[1], turn))


def own_kernel(factor, *refs):
    works, (received, _, *grads, turn) = (refs[:5], refs[5:10]), refs[10:]
    turn[...] = jnp.zeros_like(turn)
    units = received.shape[1]
    columns = pl.ds(pl.multiple_of(pl.program_id(0) * WIDE, WIDE), WIDE)
    for i, total in enumerate(slot_sums(works, slice(0, units), columns)):
        total = total + received[i, :, columns].astype(jnp.float32)
        grads[i][...] = (total * factor).astype(grads[i].dtype)


def own_grads(works, received, turn, factor, dtype):
    _, units, width = received.shape
    block = pl.BlockSpec((units, WIDE), lambda i: (0, i))
    return pl.pallas_call(
        functools.partial(own_kernel, factor),
        grid=(width // WIDE,),
        out_shape=(shape((units, width), dtype),) * 3 + (TURN,),
        in_specs=[VMEM] * 12,
        out_specs=(block,) * 3 + (VMEM,),
        compiler_params=limit(12),
        cost_estimate=cost(0, 0),
        name="own_grads",
    )(*fetched(*works[0], *works[1], received, turn))


def staged(body, name, outs, *values, flops=0):
    def kernel(*refs):
        refs[-1][...] = jnp.zeros(TURN.shape, TURN.dtype)
        body(*refs[: len(values) - 1], *refs[len(values) : -1])

    return pl.pallas_call(
        kernel,
        out_shape=(*outs, TURN),
        in_specs=[VMEM] * len(values),
        out_specs=(VMEM,) * (len(outs) + 1),
        compiler_params=limit(4),
        cost_estimate=cost(flops, 0),
        name=name,
    )(*fetched(*values))


def split_body(*refs):
    levels, (x, e) = refs[:-2], refs[-2:]
    rows = levels[0].shape[1]
    for i, level in enumerate(levels):
        x[i * rows : (i + 1) * rows] = level[0]
        e[i * rows : (i + 1) * rows] = level[1]


def pair_body(x, x_side, e, e_side, x_pair, e_pair):
    rows = x.shape[0]
    for out, near, side in ((x_pair, x, x_side), (e_pair, e, e_side)):
        out[:rows] = near[...]
        out[rows:] = side[...]


def first_pair_body(x, x_side, e, e_side, up, down, x_pair, e_pair, rows):
    pair_body(x, x_side, e, e_side, x_pair, e_pair)
    rows[0] = x[...]
    rows[1] = e[...]


def turn_body(*refs):
    near, other, turned = refs[:3], refs[3:6], refs[6:]
    for panels, into in zip((near, other), turned):
        for i, panel in enumerate(panels):
            for at in range(0, panel.shape[1], PANEL):
                into[i, at : at + PANEL] = panel[:, at : at + PANEL].T


def pack_body(x_pair, x_far, e_pair, e_far, plane):
    rows = x_pair.shape[0]
    for i, part in enumerate((x_pair, x_far, e_pair, e_far)):
        plane[i * rows : (i + 1) * rows] = part[...]


def spread_body(rows, gate, x, e):
    x[...] = rows[0]
    e[...] = rows[1]


def plane_body(out_keep, out_far, row_keep, row_far, out_mid, out_side, row_mid, row_side):
    rows = out_mid.shape[0]
    for keep, far, mid, side in (
        (out_keep, out_far, out_mid, out_side),
        (row_keep, row_far, row_mid, row_side),
    ):
        mid[...] = keep[:rows] + far[:rows].astype(jnp.float32)
        side[...] = half(keep[rows:] + far[rows:].astype(jnp.float32))


def line_body(out_mid, out_side, row_mid, row_side, first, second):
    rows = first.shape[1]
    for i, (mid, side) in enumerate(((out_mid, out_side), (row_mid, row_side))):
        total = mid[...] + side[...].astype(jnp.float32)
        first[i] = total[:rows].astype(first.dtype)
        second[i] = total[rows:].astype(second.dtype)


def relay_body(own, passed, total):
    total[...] = half(own[...] + passed[...].astype(jnp.float32))


def near_body(own, three, total):
    total[...] = own[...] + three[...].astype(jnp.float32)


def final_body(total, one, weight, expert_out, grad_rows):
    out, row = (total[i] + one[i].astype(jnp.float32) for i in (0, 1))
    expert_out[...] = half(weight[:, :1] * out)
    grad_rows[...] = half(row)


def shards(tokens, slot_token, slot_count, slot_gate, grad_out, w_gate, w_up, w_down):
    capacity = slot_gate.shape[0]
    devices = lax.axis_size("dp")
    all_bits = devices.bit_length() - 1
    core, along_x, along_y = 1 << CORE, 1 << LINK_X, 1 << LINK_Y
    far_bits = range(ROW_BITS + 1, all_bits)

    weights = [w_gate, w_up, w_down]
    for bit in far_bits:
        weights = [jnp.concatenate([w, swapped(w, 1 << bit)], 0) for w in weights]
    own, weight, turn = pick(tokens, slot_token, slot_count, slot_gate, grad_out)
    other = [swapped(w, core) for w in weights]

    width = own.shape[2]
    rows = 2 * capacity

    def sides_of(x, e):
        return x, swapped(x, along_x), e, swapped(e, along_y)

    def fars_of(x, e):
        return x, swapped(x, along_y), e, swapped(e, along_x)

    two = shifted(own, 2)
    one_level, two_levels = [held((capacity, width))] * 2, [held((rows, width))] * 2
    x, e, turn = staged(spread_body, "spread", one_level, own, other[0], turn, flops=C_COPY)
    x, e, own, turn = staged(
        first_pair_body, "pair_0", [*two_levels, held(own.shape)], *sides_of(x, e), *other[1:], turn
    )
    one = shifted(own, 1)
    part_0 = fars_of(x, e)
    x, e, turn = staged(split_body, "split_2", one_level, two, turn, flops=C_FIRST)
    sides_2 = sides_of(x, e)
    plane, turn = staged(pack_body, "pack", [held((4 * rows, width))], *part_0, turn, flops=C_PACK)
    part_3 = (shifted(plane, -1),)
    x, e, turn = staged(pair_body, "pair_2", two_levels, *sides_2, turn, flops=C_PAIR_FIRST)
    part_2 = fars_of(x, e)
    x, e, turn = staged(split_body, "split_1", one_level, one, turn, flops=C_LAST)
    sides_1 = sides_of(x, e)
    turned = held((3, *weights[0].shape[::-1]))
    near_turned, other_turned, turn = staged(
        turn_body, "turn_panels", [turned] * 2, *weights, *other, turn, flops=C_TURN
    )
    panels = (*weights, *other, near_turned, other_turned)
    x, e, turn = staged(pair_body, "pair_1", two_levels, *sides_1, turn, flops=C_PAIR_LAST)
    part_1 = fars_of(x, e)

    works, sides = [], []
    for parts in ((part_0, part_2), (part_1, part_3)):
        *work, out_keep, out_send, row_keep, row_send, turn = expert(parts, panels, turn)
        works.append(work)
        sides.append((out_keep, swapped(out_send, along_y), row_keep, swapped(row_send, along_x)))

    whole, piece = held((rows, width), jnp.float32), held((rows, width))

    def plane_sum(side, turn, flops=0):
        out_mid, out_side, row_mid, row_side, turn = staged(
            plane_body, "plane_sum", [whole, piece, whole, piece], *side, turn, flops=flops
        )
        return (out_mid, swapped(out_side, along_x), row_mid, swapped(row_side, along_y)), turn

    def line_sum(middle, turn, first, flops=0):
        level_dims = (2, capacity, width)
        return staged(
            line_body, "line_sum", [held(level_dims, first), held(level_dims)], *middle, turn,
            flops=flops,
        )

    middle_02, turn = plane_sum(sides[0], turn)
    sent, turn = other_grads(works, turn)
    received = swapped(sent, core)
    middle_31, turn = plane_sum(sides[1], turn, LONG)
    sum_0, sum_2, turn = line_sum(middle_02, turn, jnp.float32)
    passed = shifted(sum_2, -1)
    sum_1, sum_3, turn = line_sum(middle_31, turn, jnp.float32)
    three = shifted(sum_3, 1)
    factor = 1.0 / math.sqrt(devices * capacity)
    if far_bits:
        *owned, turn = own_grads(works, received, turn, 1.0, jnp.float32)
        for bit in reversed(far_bits):
            cut = owned[0].shape[0] // 2
            owned = [t[:cut] + swapped(half(t[cut:]), 1 << bit) for t in owned]
        owned = [half(total * factor) for total in owned]
    else:
        *owned, turn = own_grads(works, received, turn, factor, jnp.bfloat16)
    sum_1, turn = staged(relay_body, "relay", [held(own.shape)], sum_1, passed, turn)
    one = shifted(sum_1, -1)
    total, turn = staged(
        near_body, "near_sum", [held(own.shape, jnp.float32)], sum_0, three, turn, flops=LONG // 10
    )
    expert_out, grad_rows, turn = staged(
        final_body, "final", [shape((capacity, width))] * 2, total, one, weight, turn
    )
    return (expert_out, grad_rows, *owned)


def solution(mesh):
    return jax.shard_map(
        shards,
        mesh=mesh,
        in_specs=(
            P("dp", None),
            P("dp"),
            P(),
            P("dp"),
            P("dp", None),
            P("dp", None),
            P("dp", None),
            P("dp", None),
        ),
        out_specs=(P("dp", None), P("dp", None), P("dp", None), P("dp", None), P("dp", None)),
        check_vma=False,
    )
```

```python
import functools
import math

import jax
import jax.numpy as jnp
from jax import lax
from jax.experimental import pallas as pl
from jax.experimental.pallas import tpu as pltpu
from jax.sharding import PartitionSpec as P

CORE, LINK_X, LINK_Y, LINK_Z = 0, 1, 2, 3
ROW_BITS = 4
LONG = 10**11
C_PACK = 0
C_PAIR_FIRST = 0
C_FIRST = LONG * 4 // 100
C_LAST = LONG * 3 // 100
C_PAIR_LAST = LONG // 100
C_COPY = LONG // 5
C_TURN = 0
C_LOAD = LONG // 5
PANEL = 512
WIDE = 1536
FIRST_GRADS, LAST_GRADS = (0,), (1, 2)
TURN = pltpu.VMEM((8, 128), jnp.float32)
VMEM = pl.BlockSpec(memory_space=pltpu.VMEM)
HBM = pl.BlockSpec(memory_space=pltpu.HBM)
SMEM = pl.BlockSpec(memory_space=pltpu.SMEM)


def swapped(block, mask):
    count = lax.axis_size("dp")
    return lax.ppermute(block, "dp", [(low, low ^ mask) for low in range(count)])


def shifted(block, steps):
    count = lax.axis_size("dp")
    span = 1 << (ROW_BITS + 1)
    rise = (steps << LINK_Z) % span
    route = [(low, low // span * span + (low + rise) % span) for low in range(count)]
    return lax.ppermute(block, "dp", route)


def row_product(left, right):
    return lax.dot_general(
        left, right, (((1,), (1,)), ((), ())), preferred_element_type=jnp.float32
    )


def col_product(left, right):
    return lax.dot_general(
        left, right, (((0,), (0,)), ((), ())), preferred_element_type=jnp.float32
    )


def product(left, right):
    return jnp.dot(left, right, preferred_element_type=jnp.float32)


def half(value):
    return value.astype(jnp.bfloat16)


def shape(dims, dtype=jnp.bfloat16):
    return jax.ShapeDtypeStruct(dims, dtype)


def held(dims, dtype=jnp.bfloat16):
    return pltpu.VMEM(dims, dtype)


def fetched(*values):
    return [pltpu.with_memory_space_constraint(value, pltpu.VMEM) for value in values]


def in_hbm(value):
    return pltpu.with_memory_space_constraint(value, pltpu.HBM)


def limit(mib):
    return pltpu.CompilerParams(vmem_limit_bytes=mib << 20)


def cost(flops, moved):
    return pl.CostEstimate(flops=flops, bytes_accessed=moved, transcendentals=0)


def pick_kernel(
    place, token, count, gate, tokens, grad, rows, weight, turn,
    token_here, count_here, gate_here, tokens_here, grad_here, arrived,
):
    pairs = (
        (token, token_here),
        (count, count_here),
        (gate, gate_here),
        (tokens, tokens_here),
        (grad, grad_here),
    )
    copies = [pltpu.make_async_copy(*pair, arrived.at[i]) for i, pair in enumerate(pairs)]
    for copy in copies:
        copy.start()
    turn[...] = jnp.zeros_like(turn)
    for copy in copies:
        copy.wait()
    capacity, lanes = weight.shape
    row = lax.broadcasted_iota(jnp.int32, (capacity, lanes), 0)
    live = count_here[place[0]]
    index = jnp.zeros((capacity, lanes), jnp.int32)
    scale = jnp.zeros((capacity, lanes), jnp.float32)
    for slot in range(capacity):
        index = jnp.where(row == slot, token_here[slot], index)
        scale = jnp.where(row == slot, jnp.where(slot < live, gate_here[slot], 0.0), scale)
    weight[...] = scale
    lane = lax.broadcasted_iota(jnp.int32, (capacity, tokens.shape[0]), 1)
    chosen = jnp.where(lane == index[:, :1], 1.0, 0.0).astype(jnp.bfloat16)
    rows[0] = half(product(chosen, tokens_here[...]))
    rows[1] = half(scale[:, :1] * grad_here[...].astype(jnp.float32))


def pick(tokens, slot_token, slot_count, slot_gate, grad_out):
    capacity, width = grad_out.shape
    inputs = (slot_token, slot_count, slot_gate, tokens, grad_out)
    return pl.pallas_call(
        pick_kernel,
        out_shape=(
            held((2, capacity, width)),
            held((capacity, 128), jnp.float32),
            TURN,
        ),
        in_specs=[SMEM] + [HBM] * 5,
        out_specs=(VMEM,) * 3,
        scratch_shapes=[pltpu.SMEM(v.shape, v.dtype) for v in inputs[:3]]
        + [pltpu.VMEM(v.shape, v.dtype) for v in inputs[3:]]
        + [pltpu.SemaphoreType.DMA((5,))],
        compiler_params=limit(4),
        cost_estimate=cost(0, 0),
        name="pick",
    )(lax.axis_index("dp")[None], *(in_hbm(v) for v in inputs))


def expert_kernel(sizes, *refs):
    parts = []
    for size in sizes:
        part, refs = refs[:size], refs[size:]
        if size == 1:
            cut = part[0].shape[0] // 4
            part = [part[0].at[i * cut : (i + 1) * cut] for i in range(4)]
        parts.append(part)
    near, other, (near_turned, other_turned, _) = refs[:3], refs[3:6], refs[6:9]
    refs = refs[9:]
    x, e, hidden, gate_grad, up_grad, out_keep, out_send, row_keep, row_send, turn = refs
    turn[...] = jnp.zeros_like(turn)
    units = near[0].shape[0]
    rows = x.shape[0] // 4
    size = rows // len(parts)
    for i, (x_pair, x_far, e_pair, e_far) in enumerate(parts):
        for plane, (x_from, e_from, x_half, e_half) in enumerate(
            ((x_pair, e_pair, 0, 0), (x_pair, e_far, 1, 0), (x_far, e_pair, 0, 1), (x_far, e_far, 1, 1))
        ):
            into = slice(plane * rows + i * size, plane * rows + (i + 1) * size)
            x[into] = x_from[x_half * size : (x_half + 1) * size]
            e[into] = e_from[e_half * size : (e_half + 1) * size]
    for i, panels in enumerate((near_turned, other_turned)):
        mine = slice(i * units, (i + 1) * units)
        gate_pre = product(x[...], panels[0])
        up_pre = product(x[...], panels[1])
        hidden_grad = product(e[...], panels[2])
        gate_sig = jax.nn.sigmoid(gate_pre)
        activated = gate_pre * gate_sig
        hidden[:, mine] = half(activated * up_pre)
        gate_grad[:, mine] = half(
            hidden_grad * up_pre * (gate_sig * (1.0 + gate_pre * (1.0 - gate_sig)))
        )
        up_grad[:, mine] = half(hidden_grad * activated)
    for at in range(0, x.shape[1], PANEL):
        part = slice(at, at + PANEL)
        out = product(hidden[:, :units], near[2][:, part]) + product(
            hidden[:, units:], other[2][:, part]
        )
        out_keep[:, part] = out[: 2 * rows]
        out_send[:, part] = half(out[2 * rows :])
        row = (
            product(gate_grad[:, :units], near[0][:, part])
            + product(gate_grad[:, units:], other[0][:, part])
            + product(up_grad[:, :units], near[1][:, part])
            + product(up_grad[:, units:], other[1][:, part])
        )
        row_keep[:rows, part] = row[:rows]
        row_keep[rows:, part] = row[2 * rows : 3 * rows]
        row_send[:rows, part] = half(row[rows : 2 * rows])
        row_send[rows:, part] = half(row[3 * rows :])


def expert(parts, panels, turn):
    rows = sum(ref.shape[0] for part in parts for ref in part) // 2
    width = parts[0][0].shape[1]
    units = 2 * panels[0].shape[0]
    saved, kept, sent = (
        held((rows, units)),
        held((rows // 2, width), jnp.float32),
        held((rows // 2, width)),
    )
    return pl.pallas_call(
        functools.partial(expert_kernel, [len(part) for part in parts]),
        out_shape=(held((rows, width)),) * 2 + (saved,) * 3 + (kept, sent, kept, sent, TURN),
        in_specs=[VMEM] * (sum(len(part) for part in parts) + 9),
        out_specs=(VMEM,) * 10,
        compiler_params=limit(12),
        cost_estimate=cost(12 * rows * units * width, 6 * units * width),
        name="expert",
    )(*fetched(*(ref for part in parts for ref in part), *panels, turn))


def slot_sum(works, which, units, columns):
    left, right = ((3, 0), (4, 0), (2, 1))[which]
    return col_product(
        jnp.concatenate([refs[left][:, units] for refs in works], 0),
        jnp.concatenate([refs[right][:, columns] for refs in works], 0),
    )


def other_kernel(*refs):
    works, (_, grads, turn) = (refs[:5], refs[5:10]), refs[10:]
    turn[...] = jnp.zeros_like(turn)
    units = grads.shape[1]
    for at in range(0, grads.shape[2], PANEL):
        columns = slice(at, at + PANEL)
        for i in range(3):
            grads[i, :, columns] = half(slot_sum(works, i, slice(units, 2 * units), columns))


def other_grads(works, turn):
    width = works[0][0].shape[1]
    units = works[0][2].shape[1] // 2
    return pl.pallas_call(
        other_kernel,
        out_shape=(held((3, units, width)), TURN),
        in_specs=[VMEM] * 11,
        out_specs=(VMEM, VMEM),
        compiler_params=limit(8),
        cost_estimate=cost(LONG // 50, 0),
        name="other_grads",
    )(*fetched(*works[0], *works[1], turn))


def own_kernel(which, factor, *refs):
    works, (received, _, *grads, turn) = (refs[:5], refs[5:10]), refs[10:]
    turn[...] = jnp.zeros_like(turn)
    units = received.shape[1]
    columns = pl.ds(pl.multiple_of(pl.program_id(0) * WIDE, WIDE), WIDE)
    for i, grad in zip(which, grads):
        total = slot_sum(works, i, slice(0, units), columns)
        total = total + received[i, :, columns].astype(jnp.float32)
        grad[...] = (total * factor).astype(grad.dtype)


def own_grads(which, works, received, turn, factor, dtype):
    _, units, width = received.shape
    block = pl.BlockSpec((units, WIDE), lambda i: (0, i))
    return pl.pallas_call(
        functools.partial(own_kernel, which, factor),
        grid=(width // WIDE,),
        out_shape=(shape((units, width), dtype),) * len(which) + (TURN,),
        in_specs=[VMEM] * 12,
        out_specs=(block,) * len(which) + (VMEM,),
        compiler_params=limit(12),
        cost_estimate=cost(0, 0),
        name="own_grads",
    )(*fetched(*works[0], *works[1], received, turn))


def staged(body, name, outs, *values, flops=0):
    def kernel(*refs):
        refs[-1][...] = jnp.zeros(TURN.shape, TURN.dtype)
        body(*refs[: len(values) - 1], *refs[len(values) : -1])

    return pl.pallas_call(
        kernel,
        out_shape=(*outs, TURN),
        in_specs=[VMEM] * len(values),
        out_specs=(VMEM,) * (len(outs) + 1),
        compiler_params=limit(4),
        cost_estimate=cost(flops, 0),
        name=name,
    )(*fetched(*values))


def split_body(*refs):
    levels, (x, e) = refs[:-2], refs[-2:]
    rows = levels[0].shape[1]
    for i, level in enumerate(levels):
        x[i * rows : (i + 1) * rows] = level[0]
        e[i * rows : (i + 1) * rows] = level[1]


def pair_body(x, x_side, e, e_side, x_pair, e_pair):
    rows = x.shape[0]
    for out, near, side in ((x_pair, x, x_side), (e_pair, e, e_side)):
        out[:rows] = near[...]
        out[rows:] = side[...]


def first_pair_body(x, x_side, e, e_side, up, down, x_pair, e_pair, rows):
    pair_body(x, x_side, e, e_side, x_pair, e_pair)
    rows[0] = x[...]
    rows[1] = e[...]


def turn_body(*refs):
    near, other, turned = refs[:3], refs[3:6], refs[6:]
    for panels, into in zip((near, other), turned):
        for i, panel in enumerate(panels):
            for at in range(0, panel.shape[1], PANEL):
                into[i, at : at + PANEL] = panel[:, at : at + PANEL].T


def pack_body(x_pair, x_far, e_pair, e_far, plane):
    rows = x_pair.shape[0]
    for i, part in enumerate((x_pair, x_far, e_pair, e_far)):
        plane[i * rows : (i + 1) * rows] = part[...]


def spread_body(rows, gate, x, e):
    x[...] = rows[0]
    e[...] = rows[1]


def plane_body(out_keep, out_far, row_keep, row_far, out_mid, out_side, row_mid, row_side):
    rows = out_mid.shape[0]
    for keep, far, mid, side in (
        (out_keep, out_far, out_mid, out_side),
        (row_keep, row_far, row_mid, row_side),
    ):
        mid[...] = keep[:rows] + far[:rows].astype(jnp.float32)
        side[...] = half(keep[rows:] + far[rows:].astype(jnp.float32))


def line_body(out_mid, out_side, row_mid, row_side, first, second):
    rows = first.shape[1]
    for i, (mid, side) in enumerate(((out_mid, out_side), (row_mid, row_side))):
        total = mid[...] + side[...].astype(jnp.float32)
        first[i] = total[:rows].astype(first.dtype)
        second[i] = total[rows:].astype(second.dtype)


def relay_body(own, passed, total):
    total[...] = half(own[...] + passed[...].astype(jnp.float32))


def near_body(own, three, total):
    total[...] = own[...] + three[...].astype(jnp.float32)


def final_body(total, one, weight, expert_out, grad_rows):
    out, row = (total[i] + one[i].astype(jnp.float32) for i in (0, 1))
    expert_out[...] = half(weight[:, :1] * out)
    grad_rows[...] = half(row)


def shards(tokens, slot_token, slot_count, slot_gate, grad_out, w_gate, w_up, w_down):
    capacity = slot_gate.shape[0]
    devices = lax.axis_size("dp")
    all_bits = devices.bit_length() - 1
    core, along_x, along_y = 1 << CORE, 1 << LINK_X, 1 << LINK_Y
    far_bits = range(ROW_BITS + 1, all_bits)

    weights = [w_gate, w_up, w_down]
    for bit in far_bits:
        weights = [jnp.concatenate([w, swapped(w, 1 << bit)], 0) for w in weights]
    own, weight, turn = pick(tokens, slot_token, slot_count, slot_gate, grad_out)
    other = [swapped(w, core) for w in weights]

    width = own.shape[2]
    rows = 2 * capacity

    def sides_of(x, e):
        return x, swapped(x, along_x), e, swapped(e, along_y)

    def fars_of(x, e):
        return x, swapped(x, along_y), e, swapped(e, along_x)

    two = shifted(own, 2)
    one_level, two_levels = [held((capacity, width))] * 2, [held((rows, width))] * 2
    x, e, turn = staged(spread_body, "spread", one_level, own, other[0], turn, flops=C_COPY)
    x, e, own, turn = staged(
        first_pair_body, "pair_0", [*two_levels, held(own.shape)], *sides_of(x, e), *other[1:], turn
    )
    one = shifted(own, 1)
    part_0 = fars_of(x, e)
    x, e, turn = staged(split_body, "split_2", one_level, two, turn, flops=C_FIRST)
    sides_2 = sides_of(x, e)
    plane, turn = staged(pack_body, "pack", [held((4 * rows, width))], *part_0, turn, flops=C_PACK)
    part_3 = (shifted(plane, -1),)
    x, e, turn = staged(pair_body, "pair_2", two_levels, *sides_2, turn, flops=C_PAIR_FIRST)
    part_2 = fars_of(x, e)
    x, e, turn = staged(split_body, "split_1", one_level, one, turn, flops=C_LAST)
    sides_1 = sides_of(x, e)
    turned = held((3, *weights[0].shape[::-1]))
    near_turned, other_turned, turn = staged(
        turn_body, "turn_panels", [turned] * 2, *weights, *other, turn, flops=C_TURN
    )
    panels = (*weights, *other, near_turned, other_turned)
    x, e, turn = staged(pair_body, "pair_1", two_levels, *sides_1, turn, flops=C_PAIR_LAST)
    part_1 = fars_of(x, e)

    works, sides = [], []
    for parts in ((part_0, part_2), (part_1, part_3)):
        *work, out_keep, out_send, row_keep, row_send, turn = expert(parts, panels, turn)
        works.append(work)
        sides.append((out_keep, swapped(out_send, along_y), row_keep, swapped(row_send, along_x)))

    whole, piece = held((rows, width), jnp.float32), held((rows, width))

    def plane_sum(side, turn, flops=0):
        out_mid, out_side, row_mid, row_side, turn = staged(
            plane_body, "plane_sum", [whole, piece, whole, piece], *side, turn, flops=flops
        )
        return (out_mid, swapped(out_side, along_x), row_mid, swapped(row_side, along_y)), turn

    def line_sum(middle, turn, first, flops=0):
        level_dims = (2, capacity, width)
        return staged(
            line_body, "line_sum", [held(level_dims, first), held(level_dims)], *middle, turn,
            flops=flops,
        )

    middle_02, turn = plane_sum(sides[0], turn)
    sent, turn = other_grads(works, turn)
    received = swapped(sent, core)
    middle_31, turn = plane_sum(sides[1], turn, LONG)
    sum_0, sum_2, turn = line_sum(middle_02, turn, jnp.float32)
    passed = shifted(sum_2, -1)
    sum_1, sum_3, turn = line_sum(middle_31, turn, jnp.float32)
    three = shifted(sum_3, 1)
    factor = 1.0 / math.sqrt(devices * capacity)
    scale, dtype = (1.0, jnp.float32) if far_bits else (factor, jnp.bfloat16)
    *owned, turn = own_grads(FIRST_GRADS, works, received, turn, scale, dtype)
    sum_1, turn = staged(relay_body, "relay", [held(own.shape)], sum_1, passed, turn)
    one = shifted(sum_1, -1)
    *rest, turn = own_grads(LAST_GRADS, works, received, turn, scale, dtype)
    owned += rest
    if far_bits:
        for bit in reversed(far_bits):
            cut = owned[0].shape[0] // 2
            owned = [t[:cut] + swapped(half(t[cut:]), 1 << bit) for t in owned]
        owned = [half(total * factor) for total in owned]
    total, turn = staged(
        near_body, "near_sum", [held(own.shape, jnp.float32)], sum_0, three, turn, flops=LONG // 10
    )
    expert_out, grad_rows, turn = staged(
        final_body, "final", [shape((capacity, width))] * 2, total, one, weight, turn
    )
    return (expert_out, grad_rows, *owned)


def solution(mesh):
    return jax.shard_map(
        shards,
        mesh=mesh,
        in_specs=(
            P("dp", None),
            P("dp"),
            P(),
            P("dp"),
            P("dp", None),
            P("dp", None),
            P("dp", None),
            P("dp", None),
        ),
        out_specs=(P("dp", None), P("dp", None), P("dp", None), P("dp", None), P("dp", None)),
        check_vma=False,
    )
```

```python
import functools
import math

import jax
import jax.numpy as jnp
from jax import lax
from jax.experimental import pallas as pl
from jax.experimental.pallas import tpu as pltpu
from jax.sharding import PartitionSpec as P

CORE, LINK_X, LINK_Y, LINK_Z = 0, 1, 2, 3
ROW_BITS = 4
LONG = 10**11
C_PACK = 0
C_PAIR_FIRST = 0
C_FIRST = LONG * 4 // 100
C_LAST = LONG * 3 // 100
C_PAIR_LAST = LONG // 100
C_COPY = LONG // 5
C_TURN = 0
C_LOAD = LONG // 5
PANEL = 512
WIDE = 1536
FIRST_GRADS, LAST_GRADS = (0,), (1, 2)
TURN = pltpu.VMEM((8, 128), jnp.float32)
VMEM = pl.BlockSpec(memory_space=pltpu.VMEM)
HBM = pl.BlockSpec(memory_space=pltpu.HBM)
SMEM = pl.BlockSpec(memory_space=pltpu.SMEM)


def swapped(block, mask):
    count = lax.axis_size("dp")
    return lax.ppermute(block, "dp", [(low, low ^ mask) for low in range(count)])


def shifted(block, steps):
    count = lax.axis_size("dp")
    span = 1 << (ROW_BITS + 1)
    rise = (steps << LINK_Z) % span
    route = [(low, low // span * span + (low + rise) % span) for low in range(count)]
    return lax.ppermute(block, "dp", route)


def row_product(left, right):
    return lax.dot_general(
        left, right, (((1,), (1,)), ((), ())), preferred_element_type=jnp.float32
    )


def col_product(left, right):
    return lax.dot_general(
        left, right, (((0,), (0,)), ((), ())), preferred_element_type=jnp.float32
    )


def product(left, right):
    return jnp.dot(left, right, preferred_element_type=jnp.float32)


def half(value):
    return value.astype(jnp.bfloat16)


def shape(dims, dtype=jnp.bfloat16):
    return jax.ShapeDtypeStruct(dims, dtype)


def held(dims, dtype=jnp.bfloat16):
    return pltpu.VMEM(dims, dtype)


def fetched(*values):
    return [pltpu.with_memory_space_constraint(value, pltpu.VMEM) for value in values]


def in_hbm(value):
    return pltpu.with_memory_space_constraint(value, pltpu.HBM)


def limit(mib):
    return pltpu.CompilerParams(vmem_limit_bytes=mib << 20)


def cost(flops, moved):
    return pl.CostEstimate(flops=flops, bytes_accessed=moved, transcendentals=0)


def pick_kernel(
    place, token, count, gate, tokens, grad, rows, weight, turn,
    token_here, count_here, gate_here, tokens_here, grad_here, arrived,
):
    pairs = (
        (token, token_here),
        (count, count_here),
        (gate, gate_here),
        (tokens, tokens_here),
        (grad, grad_here),
    )
    copies = [pltpu.make_async_copy(*pair, arrived.at[i]) for i, pair in enumerate(pairs)]
    for copy in copies:
        copy.start()
    turn[...] = jnp.zeros_like(turn)
    for copy in copies[:3]:
        copy.wait()
    capacity, lanes = weight.shape
    row = lax.broadcasted_iota(jnp.int32, (capacity, lanes), 0)
    live = count_here[place[0]]
    index = jnp.zeros((capacity, lanes), jnp.int32)
    scale = jnp.zeros((capacity, lanes), jnp.float32)
    for slot in range(capacity):
        index = jnp.where(row == slot, token_here[slot], index)
        scale = jnp.where(row == slot, jnp.where(slot < live, gate_here[slot], 0.0), scale)
    weight[...] = scale
    lane = lax.broadcasted_iota(jnp.int32, (capacity, tokens.shape[0]), 1)
    chosen = jnp.where(lane == index[:, :1], 1.0, 0.0).astype(jnp.bfloat16)
    copies[3].wait()
    rows[0] = half(product(chosen, tokens_here[...]))
    copies[4].wait()
    rows[1] = half(scale[:, :1] * grad_here[...].astype(jnp.float32))


def pick(tokens, slot_token, slot_count, slot_gate, grad_out):
    capacity, width = grad_out.shape
    inputs = (slot_token, slot_count, slot_gate, tokens, grad_out)
    return pl.pallas_call(
        pick_kernel,
        out_shape=(
            held((2, capacity, width)),
            held((capacity, 128), jnp.float32),
            TURN,
        ),
        in_specs=[SMEM] + [HBM] * 5,
        out_specs=(VMEM,) * 3,
        scratch_shapes=[pltpu.SMEM(v.shape, v.dtype) for v in inputs[:3]]
        + [pltpu.VMEM(v.shape, v.dtype) for v in inputs[3:]]
        + [pltpu.SemaphoreType.DMA((5,))],
        compiler_params=limit(4),
        cost_estimate=cost(0, 0),
        name="pick",
    )(lax.axis_index("dp")[None], *(in_hbm(v) for v in inputs))


def expert_kernel(sizes, *refs):
    parts = []
    for size in sizes:
        part, refs = refs[:size], refs[size:]
        if size == 1:
            cut = part[0].shape[0] // 4
            part = [part[0].at[i * cut : (i + 1) * cut] for i in range(4)]
        parts.append(part)
    near, other, (near_turned, other_turned, _) = refs[:3], refs[3:6], refs[6:9]
    refs = refs[9:]
    x, e, hidden, gate_grad, up_grad, out_keep, out_send, row_keep, row_send, turn = refs
    turn[...] = jnp.zeros_like(turn)
    units = near[0].shape[0]
    rows = x.shape[0] // 4
    size = rows // len(parts)
    for i, (x_pair, x_far, e_pair, e_far) in enumerate(parts):
        for plane, (x_from, e_from, x_half, e_half) in enumerate(
            ((x_pair, e_pair, 0, 0), (x_pair, e_far, 1, 0), (x_far, e_pair, 0, 1), (x_far, e_far, 1, 1))
        ):
            into = slice(plane * rows + i * size, plane * rows + (i + 1) * size)
            x[into] = x_from[x_half * size : (x_half + 1) * size]
            e[into] = e_from[e_half * size : (e_half + 1) * size]
    for i, panels in enumerate((near_turned, other_turned)):
        mine = slice(i * units, (i + 1) * units)
        gate_pre = product(x[...], panels[0])
        up_pre = product(x[...], panels[1])
        hidden_grad = product(e[...], panels[2])
        gate_sig = jax.nn.sigmoid(gate_pre)
        activated = gate_pre * gate_sig
        hidden[:, mine] = half(activated * up_pre)
        gate_grad[:, mine] = half(
            hidden_grad * up_pre * (gate_sig * (1.0 + gate_pre * (1.0 - gate_sig)))
        )
        up_grad[:, mine] = half(hidden_grad * activated)
    for at in range(0, x.shape[1], PANEL):
        part = slice(at, at + PANEL)
        out = product(hidden[:, :units], near[2][:, part]) + product(
            hidden[:, units:], other[2][:, part]
        )
        out_keep[:, part] = out[: 2 * rows]
        out_send[:, part] = half(out[2 * rows :])
        row = (
            product(gate_grad[:, :units], near[0][:, part])
            + product(gate_grad[:, units:], other[0][:, part])
            + product(up_grad[:, :units], near[1][:, part])
            + product(up_grad[:, units:], other[1][:, part])
        )
        row_keep[:rows, part] = row[:rows]
        row_keep[rows:, part] = row[2 * rows : 3 * rows]
        row_send[:rows, part] = half(row[rows : 2 * rows])
        row_send[rows:, part] = half(row[3 * rows :])


def expert(parts, panels, turn):
    rows = sum(ref.shape[0] for part in parts for ref in part) // 2
    width = parts[0][0].shape[1]
    units = 2 * panels[0].shape[0]
    saved, kept, sent = (
        held((rows, units)),
        held((rows // 2, width), jnp.float32),
        held((rows // 2, width)),
    )
    return pl.pallas_call(
        functools.partial(expert_kernel, [len(part) for part in parts]),
        out_shape=(held((rows, width)),) * 2 + (saved,) * 3 + (kept, sent, kept, sent, TURN),
        in_specs=[VMEM] * (sum(len(part) for part in parts) + 9),
        out_specs=(VMEM,) * 10,
        compiler_params=limit(12),
        cost_estimate=cost(12 * rows * units * width, 6 * units * width),
        name="expert",
    )(*fetched(*(ref for part in parts for ref in part), *panels, turn))


def slot_sum(works, which, units, columns):
    left, right = ((3, 0), (4, 0), (2, 1))[which]
    return col_product(
        jnp.concatenate([refs[left][:, units] for refs in works], 0),
        jnp.concatenate([refs[right][:, columns] for refs in works], 0),
    )


def other_kernel(*refs):
    works, (_, grads, turn) = (refs[:5], refs[5:10]), refs[10:]
    turn[...] = jnp.zeros_like(turn)
    units = grads.shape[1]
    for at in range(0, grads.shape[2], PANEL):
        columns = slice(at, at + PANEL)
        for i in range(3):
            grads[i, :, columns] = half(slot_sum(works, i, slice(units, 2 * units), columns))


def other_grads(works, turn):
    width = works[0][0].shape[1]
    units = works[0][2].shape[1] // 2
    return pl.pallas_call(
        other_kernel,
        out_shape=(held((3, units, width)), TURN),
        in_specs=[VMEM] * 11,
        out_specs=(VMEM, VMEM),
        compiler_params=limit(8),
        cost_estimate=cost(LONG // 50, 0),
        name="other_grads",
    )(*fetched(*works[0], *works[1], turn))


def own_kernel(which, factor, *refs):
    works, (received, _, *grads, turn) = (refs[:5], refs[5:10]), refs[10:]
    turn[...] = jnp.zeros_like(turn)
    units = received.shape[1]
    columns = pl.ds(pl.multiple_of(pl.program_id(0) * WIDE, WIDE), WIDE)
    for i, grad in zip(which, grads):
        total = slot_sum(works, i, slice(0, units), columns)
        total = total + received[i, :, columns].astype(jnp.float32)
        grad[...] = (total * factor).astype(grad.dtype)


def own_grads(which, works, received, turn, factor, dtype):
    _, units, width = received.shape
    block = pl.BlockSpec((units, WIDE), lambda i: (0, i))
    return pl.pallas_call(
        functools.partial(own_kernel, which, factor),
        grid=(width // WIDE,),
        out_shape=(shape((units, width), dtype),) * len(which) + (TURN,),
        in_specs=[VMEM] * 12,
        out_specs=(block,) * len(which) + (VMEM,),
        compiler_params=limit(12),
        cost_estimate=cost(0, 0),
        name="own_grads",
    )(*fetched(*works[0], *works[1], received, turn))


def staged(body, name, outs, *values, flops=0):
    def kernel(*refs):
        refs[-1][...] = jnp.zeros(TURN.shape, TURN.dtype)
        body(*refs[: len(values) - 1], *refs[len(values) : -1])

    return pl.pallas_call(
        kernel,
        out_shape=(*outs, TURN),
        in_specs=[VMEM] * len(values),
        out_specs=(VMEM,) * (len(outs) + 1),
        compiler_params=limit(4),
        cost_estimate=cost(flops, 0),
        name=name,
    )(*fetched(*values))


def split_body(*refs):
    levels, (x, e) = refs[:-2], refs[-2:]
    rows = levels[0].shape[1]
    for i, level in enumerate(levels):
        x[i * rows : (i + 1) * rows] = level[0]
        e[i * rows : (i + 1) * rows] = level[1]


def pair_body(x, x_side, e, e_side, x_pair, e_pair):
    rows = x.shape[0]
    for out, near, side in ((x_pair, x, x_side), (e_pair, e, e_side)):
        out[:rows] = near[...]
        out[rows:] = side[...]


def first_pair_body(x, x_side, e, e_side, up, down, x_pair, e_pair, rows):
    pair_body(x, x_side, e, e_side, x_pair, e_pair)
    rows[0] = x[...]
    rows[1] = e[...]


def turn_body(*refs):
    near, other, turned = refs[:3], refs[3:6], refs[6:]
    for panels, into in zip((near, other), turned):
        for i, panel in enumerate(panels):
            for at in range(0, panel.shape[1], PANEL):
                into[i, at : at + PANEL] = panel[:, at : at + PANEL].T


def pack_body(x_pair, x_far, e_pair, e_far, plane):
    rows = x_pair.shape[0]
    for i, part in enumerate((x_pair, x_far, e_pair, e_far)):
        plane[i * rows : (i + 1) * rows] = part[...]


def spread_body(rows, gate, x, e):
    x[...] = rows[0]
    e[...] = rows[1]


def plane_body(out_keep, out_far, row_keep, row_far, out_mid, out_side, row_mid, row_side):
    rows = out_mid.shape[0]
    for keep, far, mid, side in (
        (out_keep, out_far, out_mid, out_side),
        (row_keep, row_far, row_mid, row_side),
    ):
        mid[...] = keep[:rows] + far[:rows].astype(jnp.float32)
        side[...] = half(keep[rows:] + far[rows:].astype(jnp.float32))


def line_body(out_mid, out_side, row_mid, row_side, first, second):
    rows = first.shape[1]
    for i, (mid, side) in enumerate(((out_mid, out_side), (row_mid, row_side))):
        total = mid[...] + side[...].astype(jnp.float32)
        first[i] = total[:rows].astype(first.dtype)
        second[i] = total[rows:].astype(second.dtype)


def relay_body(own, passed, total):
    total[...] = half(own[...] + passed[...].astype(jnp.float32))


def near_body(own, three, total):
    total[...] = own[...] + three[...].astype(jnp.float32)


def final_body(total, one, weight, expert_out, grad_rows):
    out, row = (total[i] + one[i].astype(jnp.float32) for i in (0, 1))
    expert_out[...] = half(weight[:, :1] * out)
    grad_rows[...] = half(row)


def shards(tokens, slot_token, slot_count, slot_gate, grad_out, w_gate, w_up, w_down):
    capacity = slot_gate.shape[0]
    devices = lax.axis_size("dp")
    all_bits = devices.bit_length() - 1
    core, along_x, along_y = 1 << CORE, 1 << LINK_X, 1 << LINK_Y
    far_bits = range(ROW_BITS + 1, all_bits)

    weights = [w_gate, w_up, w_down]
    for bit in far_bits:
        weights = [jnp.concatenate([w, swapped(w, 1 << bit)], 0) for w in weights]
    own, weight, turn = pick(tokens, slot_token, slot_count, slot_gate, grad_out)
    other = [swapped(w, core) for w in weights]

    width = own.shape[2]
    rows = 2 * capacity

    def sides_of(x, e):
        return x, swapped(x, along_x), e, swapped(e, along_y)

    def fars_of(x, e):
        return x, swapped(x, along_y), e, swapped(e, along_x)

    two = shifted(own, 2)
    one_level, two_levels = [held((capacity, width))] * 2, [held((rows, width))] * 2
    x, e, turn = staged(spread_body, "spread", one_level, own, other[0], turn, flops=C_COPY)
    x, e, own, turn = staged(
        first_pair_body, "pair_0", [*two_levels, held(own.shape)], *sides_of(x, e), *other[1:], turn
    )
    one = shifted(own, 1)
    part_0 = fars_of(x, e)
    x, e, turn = staged(split_body, "split_2", one_level, two, turn, flops=C_FIRST)
    sides_2 = sides_of(x, e)
    plane, turn = staged(pack_body, "pack", [held((4 * rows, width))], *part_0, turn, flops=C_PACK)
    part_3 = (shifted(plane, -1),)
    x, e, turn = staged(pair_body, "pair_2", two_levels, *sides_2, turn, flops=C_PAIR_FIRST)
    part_2 = fars_of(x, e)
    x, e, turn = staged(split_body, "split_1", one_level, one, turn, flops=C_LAST)
    sides_1 = sides_of(x, e)
    turned = held((3, *weights[0].shape[::-1]))
    near_turned, other_turned, turn = staged(
        turn_body, "turn_panels", [turned] * 2, *weights, *other, turn, flops=C_TURN
    )
    panels = (*weights, *other, near_turned, other_turned)
    x, e, turn = staged(pair_body, "pair_1", two_levels, *sides_1, turn, flops=C_PAIR_LAST)
    part_1 = fars_of(x, e)

    works, sides = [], []
    for parts in ((part_0, part_2), (part_1, part_3)):
        *work, out_keep, out_send, row_keep, row_send, turn = expert(parts, panels, turn)
        works.append(work)
        sides.append((out_keep, swapped(out_send, along_y), row_keep, swapped(row_send, along_x)))

    whole, piece = held((rows, width), jnp.float32), held((rows, width))

    def plane_sum(side, turn, flops=0):
        out_mid, out_side, row_mid, row_side, turn = staged(
            plane_body, "plane_sum", [whole, piece, whole, piece], *side, turn, flops=flops
        )
        return (out_mid, swapped(out_side, along_x), row_mid, swapped(row_side, along_y)), turn

    def line_sum(middle, turn, first, flops=0):
        level_dims = (2, capacity, width)
        return staged(
            line_body, "line_sum", [held(level_dims, first), held(level_dims)], *middle, turn,
            flops=flops,
        )

    middle_02, turn = plane_sum(sides[0], turn)
    sent, turn = other_grads(works, turn)
    received = swapped(sent, core)
    middle_31, turn = plane_sum(sides[1], turn, LONG)
    sum_0, sum_2, turn = line_sum(middle_02, turn, jnp.float32)
    passed = shifted(sum_2, -1)
    sum_1, sum_3, turn = line_sum(middle_31, turn, jnp.float32)
    three = shifted(sum_3, 1)
    factor = 1.0 / math.sqrt(devices * capacity)
    scale, dtype = (1.0, jnp.float32) if far_bits else (factor, jnp.bfloat16)
    *owned, turn = own_grads(FIRST_GRADS, works, received, turn, scale, dtype)
    sum_1, turn = staged(relay_body, "relay", [held(own.shape)], sum_1, passed, turn)
    one = shifted(sum_1, -1)
    *rest, turn = own_grads(LAST_GRADS, works, received, turn, scale, dtype)
    owned += rest
    if far_bits:
        for bit in reversed(far_bits):
            cut = owned[0].shape[0] // 2
            owned = [t[:cut] + swapped(half(t[cut:]), 1 << bit) for t in owned]
        owned = [half(total * factor) for total in owned]
    total, turn = staged(
        near_body, "near_sum", [held(own.shape, jnp.float32)], sum_0, three, turn, flops=LONG // 10
    )
    expert_out, grad_rows, turn = staged(
        final_body, "final", [shape((capacity, width))] * 2, total, one, weight, turn
    )
    return (expert_out, grad_rows, *owned)


def solution(mesh):
    return jax.shard_map(
        shards,
        mesh=mesh,
        in_specs=(
            P("dp", None),
            P("dp"),
            P(),
            P("dp"),
            P("dp", None),
            P("dp", None),
            P("dp", None),
            P("dp", None),
        ),
        out_specs=(P("dp", None), P("dp", None), P("dp", None), P("dp", None), P("dp", None)),
        check_vma=False,
    )
```

```python
import functools
import math

import jax
import jax.numpy as jnp
from jax import lax
from jax.experimental import pallas as pl
from jax.experimental.pallas import tpu as pltpu
from jax.sharding import PartitionSpec as P

CORE, LINK_X, LINK_Y, LINK_Z = 0, 1, 2, 3
ROW_BITS = 4
LONG = 10**11
C_PACK = 0
C_PAIR_FIRST = 0
C_FIRST = LONG * 4 // 100
C_LAST = LONG * 3 // 100
C_PAIR_LAST = LONG // 100
C_COPY = LONG // 5
C_TURN = 0
C_LOAD = LONG // 5
PANEL = 512
WIDE = 1536
FIRST_GRADS, LAST_GRADS = (0, 1), (2,)
TURN = pltpu.VMEM((8, 128), jnp.float32)
VMEM = pl.BlockSpec(memory_space=pltpu.VMEM)
HBM = pl.BlockSpec(memory_space=pltpu.HBM)
SMEM = pl.BlockSpec(memory_space=pltpu.SMEM)


def swapped(block, mask):
    count = lax.axis_size("dp")
    return lax.ppermute(block, "dp", [(low, low ^ mask) for low in range(count)])


def shifted(block, steps):
    count = lax.axis_size("dp")
    span = 1 << (ROW_BITS + 1)
    rise = (steps << LINK_Z) % span
    route = [(low, low // span * span + (low + rise) % span) for low in range(count)]
    return lax.ppermute(block, "dp", route)


def row_product(left, right):
    return lax.dot_general(
        left, right, (((1,), (1,)), ((), ())), preferred_element_type=jnp.float32
    )


def col_product(left, right):
    return lax.dot_general(
        left, right, (((0,), (0,)), ((), ())), preferred_element_type=jnp.float32
    )


def product(left, right):
    return jnp.dot(left, right, preferred_element_type=jnp.float32)


def half(value):
    return value.astype(jnp.bfloat16)


def shape(dims, dtype=jnp.bfloat16):
    return jax.ShapeDtypeStruct(dims, dtype)


def held(dims, dtype=jnp.bfloat16):
    return pltpu.VMEM(dims, dtype)


def fetched(*values):
    return [pltpu.with_memory_space_constraint(value, pltpu.VMEM) for value in values]


def in_hbm(value):
    return pltpu.with_memory_space_constraint(value, pltpu.HBM)


def limit(mib):
    return pltpu.CompilerParams(vmem_limit_bytes=mib << 20)


def cost(flops, moved):
    return pl.CostEstimate(flops=flops, bytes_accessed=moved, transcendentals=0)


def pick_kernel(
    place, token, count, gate, tokens, grad, rows, weight, turn,
    token_here, count_here, gate_here, tokens_here, grad_here, arrived,
):
    pairs = (
        (token, token_here),
        (count, count_here),
        (gate, gate_here),
        (tokens, tokens_here),
        (grad, grad_here),
    )
    copies = [pltpu.make_async_copy(*pair, arrived.at[i]) for i, pair in enumerate(pairs)]
    for copy in copies:
        copy.start()
    turn[...] = jnp.zeros_like(turn)
    for copy in copies[:3]:
        copy.wait()
    capacity, lanes = weight.shape
    row = lax.broadcasted_iota(jnp.int32, (capacity, lanes), 0)
    live = count_here[place[0]]
    index = jnp.zeros((capacity, lanes), jnp.int32)
    scale = jnp.zeros((capacity, lanes), jnp.float32)
    for slot in range(capacity):
        index = jnp.where(row == slot, token_here[slot], index)
        scale = jnp.where(row == slot, jnp.where(slot < live, gate_here[slot], 0.0), scale)
    weight[...] = scale
    lane = lax.broadcasted_iota(jnp.int32, (capacity, tokens.shape[0]), 1)
    chosen = jnp.where(lane == index[:, :1], 1.0, 0.0).astype(jnp.bfloat16)
    copies[3].wait()
    rows[0] = half(product(chosen, tokens_here[...]))
    copies[4].wait()
    rows[1] = half(scale[:, :1] * grad_here[...].astype(jnp.float32))


def pick(tokens, slot_token, slot_count, slot_gate, grad_out):
    capacity, width = grad_out.shape
    inputs = (slot_token, slot_count, slot_gate, tokens, grad_out)
    return pl.pallas_call(
        pick_kernel,
        out_shape=(
            held((2, capacity, width)),
            held((capacity, 128), jnp.float32),
            TURN,
        ),
        in_specs=[SMEM] + [HBM] * 5,
        out_specs=(VMEM,) * 3,
        scratch_shapes=[pltpu.SMEM(v.shape, v.dtype) for v in inputs[:3]]
        + [pltpu.VMEM(v.shape, v.dtype) for v in inputs[3:]]
        + [pltpu.SemaphoreType.DMA((5,))],
        compiler_params=limit(4),
        cost_estimate=cost(0, 0),
        name="pick",
    )(lax.axis_index("dp")[None], *(in_hbm(v) for v in inputs))


def expert_kernel(sizes, *refs):
    parts = []
    for size in sizes:
        part, refs = refs[:size], refs[size:]
        if size == 1:
            cut = part[0].shape[0] // 4
            part = [part[0].at[i * cut : (i + 1) * cut] for i in range(4)]
        parts.append(part)
    near, other, (near_turned, other_turned, _) = refs[:3], refs[3:6], refs[6:9]
    refs = refs[9:]
    x, e, hidden, gate_grad, up_grad, out_keep, out_send, row_keep, row_send, turn = refs
    turn[...] = jnp.zeros_like(turn)
    units = near[0].shape[0]
    rows = x.shape[0] // 4
    size = rows // len(parts)
    for i, (x_pair, x_far, e_pair, e_far) in enumerate(parts):
        for plane, (x_from, e_from, x_half, e_half) in enumerate(
            ((x_pair, e_pair, 0, 0), (x_pair, e_far, 1, 0), (x_far, e_pair, 0, 1), (x_far, e_far, 1, 1))
        ):
            into = slice(plane * rows + i * size, plane * rows + (i + 1) * size)
            x[into] = x_from[x_half * size : (x_half + 1) * size]
            e[into] = e_from[e_half * size : (e_half + 1) * size]
    for i, panels in enumerate((near_turned, other_turned)):
        mine = slice(i * units, (i + 1) * units)
        gate_pre = product(x[...], panels[0])
        up_pre = product(x[...], panels[1])
        hidden_grad = product(e[...], panels[2])
        gate_sig = jax.nn.sigmoid(gate_pre)
        activated = gate_pre * gate_sig
        hidden[:, mine] = half(activated * up_pre)
        gate_grad[:, mine] = half(
            hidden_grad * up_pre * (gate_sig * (1.0 + gate_pre * (1.0 - gate_sig)))
        )
        up_grad[:, mine] = half(hidden_grad * activated)
    for at in range(0, x.shape[1], PANEL):
        part = slice(at, at + PANEL)
        out = product(hidden[:, :units], near[2][:, part]) + product(
            hidden[:, units:], other[2][:, part]
        )
        out_keep[:, part] = out[: 2 * rows]
        out_send[:, part] = half(out[2 * rows :])
        row = (
            product(gate_grad[:, :units], near[0][:, part])
            + product(gate_grad[:, units:], other[0][:, part])
            + product(up_grad[:, :units], near[1][:, part])
            + product(up_grad[:, units:], other[1][:, part])
        )
        row_keep[:rows, part] = row[:rows]
        row_keep[rows:, part] = row[2 * rows : 3 * rows]
        row_send[:rows, part] = half(row[rows : 2 * rows])
        row_send[rows:, part] = half(row[3 * rows :])


def expert(parts, panels, turn):
    rows = sum(ref.shape[0] for part in parts for ref in part) // 2
    width = parts[0][0].shape[1]
    units = 2 * panels[0].shape[0]
    saved, kept, sent = (
        held((rows, units)),
        held((rows // 2, width), jnp.float32),
        held((rows // 2, width)),
    )
    return pl.pallas_call(
        functools.partial(expert_kernel, [len(part) for part in parts]),
        out_shape=(held((rows, width)),) * 2 + (saved,) * 3 + (kept, sent, kept, sent, TURN),
        in_specs=[VMEM] * (sum(len(part) for part in parts) + 9),
        out_specs=(VMEM,) * 10,
        compiler_params=limit(12),
        cost_estimate=cost(12 * rows * units * width, 6 * units * width),
        name="expert",
    )(*fetched(*(ref for part in parts for ref in part), *panels, turn))


def slot_sum(works, which, units, columns):
    left, right = ((3, 0), (4, 0), (2, 1))[which]
    return col_product(
        jnp.concatenate([refs[left][:, units] for refs in works], 0),
        jnp.concatenate([refs[right][:, columns] for refs in works], 0),
    )


def other_kernel(*refs):
    works, (_, grads, turn) = (refs[:5], refs[5:10]), refs[10:]
    turn[...] = jnp.zeros_like(turn)
    units = grads.shape[1]
    for at in range(0, grads.shape[2], PANEL):
        columns = slice(at, at + PANEL)
        for i in range(3):
            grads[i, :, columns] = half(slot_sum(works, i, slice(units, 2 * units), columns))


def other_grads(works, turn):
    width = works[0][0].shape[1]
    units = works[0][2].shape[1] // 2
    return pl.pallas_call(
        other_kernel,
        out_shape=(held((3, units, width)), TURN),
        in_specs=[VMEM] * 11,
        out_specs=(VMEM, VMEM),
        compiler_params=limit(8),
        cost_estimate=cost(LONG // 50, 0),
        name="other_grads",
    )(*fetched(*works[0], *works[1], turn))


def own_kernel(which, factor, *refs):
    works, (received, _, *grads, turn) = (refs[:5], refs[5:10]), refs[10:]
    turn[...] = jnp.zeros_like(turn)
    units = received.shape[1]
    columns = pl.ds(pl.multiple_of(pl.program_id(0) * WIDE, WIDE), WIDE)
    for i, grad in zip(which, grads):
        total = slot_sum(works, i, slice(0, units), columns)
        total = total + received[i, :, columns].astype(jnp.float32)
        grad[...] = (total * factor).astype(grad.dtype)


def own_grads(which, works, received, turn, factor, dtype):
    _, units, width = received.shape
    block = pl.BlockSpec((units, WIDE), lambda i: (0, i))
    return pl.pallas_call(
        functools.partial(own_kernel, which, factor),
        grid=(width // WIDE,),
        out_shape=(shape((units, width), dtype),) * len(which) + (TURN,),
        in_specs=[VMEM] * 12,
        out_specs=(block,) * len(which) + (VMEM,),
        compiler_params=limit(12),
        cost_estimate=cost(0, 0),
        name="own_grads",
    )(*fetched(*works[0], *works[1], received, turn))


def staged(body, name, outs, *values, flops=0):
    def kernel(*refs):
        refs[-1][...] = jnp.zeros(TURN.shape, TURN.dtype)
        body(*refs[: len(values) - 1], *refs[len(values) : -1])

    return pl.pallas_call(
        kernel,
        out_shape=(*outs, TURN),
        in_specs=[VMEM] * len(values),
        out_specs=(VMEM,) * (len(outs) + 1),
        compiler_params=limit(4),
        cost_estimate=cost(flops, 0),
        name=name,
    )(*fetched(*values))


def split_body(*refs):
    levels, (x, e) = refs[:-2], refs[-2:]
    rows = levels[0].shape[1]
    for i, level in enumerate(levels):
        x[i * rows : (i + 1) * rows] = level[0]
        e[i * rows : (i + 1) * rows] = level[1]


def pair_body(x, x_side, e, e_side, x_pair, e_pair):
    rows = x.shape[0]
    for out, near, side in ((x_pair, x, x_side), (e_pair, e, e_side)):
        out[:rows] = near[...]
        out[rows:] = side[...]


def first_pair_body(x, x_side, e, e_side, up, down, x_pair, e_pair, rows):
    pair_body(x, x_side, e, e_side, x_pair, e_pair)
    rows[0] = x[...]
    rows[1] = e[...]


def turn_body(*refs):
    near, other, turned = refs[:3], refs[3:6], refs[6:]
    for panels, into in zip((near, other), turned):
        for i, panel in enumerate(panels):
            for at in range(0, panel.shape[1], PANEL):
                into[i, at : at + PANEL] = panel[:, at : at + PANEL].T


def pack_body(x_pair, x_far, e_pair, e_far, plane):
    rows = x_pair.shape[0]
    for i, part in enumerate((x_pair, x_far, e_pair, e_far)):
        plane[i * rows : (i + 1) * rows] = part[...]


def spread_body(rows, gate, x, e):
    x[...] = rows[0]
    e[...] = rows[1]


def plane_body(out_keep, out_far, row_keep, row_far, out_mid, out_side, row_mid, row_side):
    rows = out_mid.shape[0]
    for keep, far, mid, side in (
        (out_keep, out_far, out_mid, out_side),
        (row_keep, row_far, row_mid, row_side),
    ):
        mid[...] = keep[:rows] + far[:rows].astype(jnp.float32)
        side[...] = half(keep[rows:] + far[rows:].astype(jnp.float32))


def line_body(out_mid, out_side, row_mid, row_side, first, second):
    rows = first.shape[1]
    for i, (mid, side) in enumerate(((out_mid, out_side), (row_mid, row_side))):
        total = mid[...] + side[...].astype(jnp.float32)
        first[i] = total[:rows].astype(first.dtype)
        second[i] = total[rows:].astype(second.dtype)


def relay_body(own, passed, total):
    total[...] = half(own[...] + passed[...].astype(jnp.float32))


def near_body(own, three, total):
    total[...] = own[...] + three[...].astype(jnp.float32)


def final_body(total, one, weight, expert_out, grad_rows):
    out, row = (total[i] + one[i].astype(jnp.float32) for i in (0, 1))
    expert_out[...] = half(weight[:, :1] * out)
    grad_rows[...] = half(row)


def shards(tokens, slot_token, slot_count, slot_gate, grad_out, w_gate, w_up, w_down):
    capacity = slot_gate.shape[0]
    devices = lax.axis_size("dp")
    all_bits = devices.bit_length() - 1
    core, along_x, along_y = 1 << CORE, 1 << LINK_X, 1 << LINK_Y
    far_bits = range(ROW_BITS + 1, all_bits)

    weights = [w_gate, w_up, w_down]
    for bit in far_bits:
        weights = [jnp.concatenate([w, swapped(w, 1 << bit)], 0) for w in weights]
    own, weight, turn = pick(tokens, slot_token, slot_count, slot_gate, grad_out)
    other = [swapped(w, core) for w in weights]

    width = own.shape[2]
    rows = 2 * capacity

    def sides_of(x, e):
        return x, swapped(x, along_x), e, swapped(e, along_y)

    def fars_of(x, e):
        return x, swapped(x, along_y), e, swapped(e, along_x)

    two = shifted(own, 2)
    one_level, two_levels = [held((capacity, width))] * 2, [held((rows, width))] * 2
    x, e, turn = staged(spread_body, "spread", one_level, own, other[0], turn, flops=C_COPY)
    x, e, own, turn = staged(
        first_pair_body, "pair_0", [*two_levels, held(own.shape)], *sides_of(x, e), *other[1:], turn
    )
    one = shifted(own, 1)
    part_0 = fars_of(x, e)
    x, e, turn = staged(split_body, "split_2", one_level, two, turn, flops=C_FIRST)
    sides_2 = sides_of(x, e)
    plane, turn = staged(pack_body, "pack", [held((4 * rows, width))], *part_0, turn, flops=C_PACK)
    part_3 = (shifted(plane, -1),)
    x, e, turn = staged(pair_body, "pair_2", two_levels, *sides_2, turn, flops=C_PAIR_FIRST)
    part_2 = fars_of(x, e)
    x, e, turn = staged(split_body, "split_1", one_level, one, turn, flops=C_LAST)
    sides_1 = sides_of(x, e)
    turned = held((3, *weights[0].shape[::-1]))
    near_turned, other_turned, turn = staged(
        turn_body, "turn_panels", [turned] * 2, *weights, *other, turn, flops=C_TURN
    )
    panels = (*weights, *other, near_turned, other_turned)
    x, e, turn = staged(pair_body, "pair_1", two_levels, *sides_1, turn, flops=C_PAIR_LAST)
    part_1 = fars_of(x, e)

    works, sides = [], []
    for parts in ((part_0, part_2), (part_1, part_3)):
        *work, out_keep, out_send, row_keep, row_send, turn = expert(parts, panels, turn)
        works.append(work)
        sides.append((out_keep, swapped(out_send, along_y), row_keep, swapped(row_send, along_x)))

    whole, piece = held((rows, width), jnp.float32), held((rows, width))

    def plane_sum(side, turn, flops=0):
        out_mid, out_side, row_mid, row_side, turn = staged(
            plane_body, "plane_sum", [whole, piece, whole, piece], *side, turn, flops=flops
        )
        return (out_mid, swapped(out_side, along_x), row_mid, swapped(row_side, along_y)), turn

    def line_sum(middle, turn, first, flops=0):
        level_dims = (2, capacity, width)
        return staged(
            line_body, "line_sum", [held(level_dims, first), held(level_dims)], *middle, turn,
            flops=flops,
        )

    middle_02, turn = plane_sum(sides[0], turn)
    sent, turn = other_grads(works, turn)
    received = swapped(sent, core)
    middle_31, turn = plane_sum(sides[1], turn, LONG)
    sum_0, sum_2, turn = line_sum(middle_02, turn, jnp.float32)
    passed = shifted(sum_2, -1)
    sum_1, sum_3, turn = line_sum(middle_31, turn, jnp.float32)
    three = shifted(sum_3, 1)
    factor = 1.0 / math.sqrt(devices * capacity)
    scale, dtype = (1.0, jnp.float32) if far_bits else (factor, jnp.bfloat16)
    *owned, turn = own_grads(FIRST_GRADS, works, received, turn, scale, dtype)
    sum_1, turn = staged(relay_body, "relay", [held(own.shape)], sum_1, passed, turn)
    one = shifted(sum_1, -1)
    *rest, turn = own_grads(LAST_GRADS, works, received, turn, scale, dtype)
    owned += rest
    if far_bits:
        for bit in reversed(far_bits):
            cut = owned[0].shape[0] // 2
            owned = [t[:cut] + swapped(half(t[cut:]), 1 << bit) for t in owned]
        owned = [half(total * factor) for total in owned]
    total, turn = staged(
        near_body, "near_sum", [held(own.shape, jnp.float32)], sum_0, three, turn, flops=LONG // 10
    )
    expert_out, grad_rows, turn = staged(
        final_body, "final", [shape((capacity, width))] * 2, total, one, weight, turn
    )
    return (expert_out, grad_rows, *owned)


def solution(mesh):
    return jax.shard_map(
        shards,
        mesh=mesh,
        in_specs=(
            P("dp", None),
            P("dp"),
            P(),
            P("dp"),
            P("dp", None),
            P("dp", None),
            P("dp", None),
            P("dp", None),
        ),
        out_specs=(P("dp", None), P("dp", None), P("dp", None), P("dp", None), P("dp", None)),
        check_vma=False,
    )
```
